512 devices in a mesh: rows: 128 (over y, z, core), chan: 4 (over x).
Axes of the slice: x: 4, y: 8, z: 8, core: 2. Of those that a mesh axis runs over, the one named last changes fastest.
Arguments:
- field: bfloat16 [128, 1024, 1024], P('chan', 'rows'), may hold values from -6 to 6
- cotangent: bfloat16 [128, 1024, 1024], P('chan', 'rows'), may hold values from -6 to 6
- local_kernel: bfloat16 [9, 128, 128], P(None, 'chan'), may hold values from -0.1875 to 0.1875
- spectral_weight: bfloat16 [128, 128, 128, 128], P('rows', None, 'chan'), may hold values from -0.5 to 0.5
- tile_ids: int32 [1024, 16, 6], P('rows'), may hold values from 0 to 8, as said below
- tile_counts: int32 [1024, 16], P('rows'), may hold values from 2 to 6
Outputs:
- grad_field: bfloat16 [128, 1024, 1024], P('chan', 'rows')
- grad_spectral: bfloat16 [128, 128, 128, 128], P('rows', None, 'chan')
- grad_kernel: float32 [9, 128, 128], P(None, 'chan')
The draws below stay inside these ranges and needn't reach their ends.
Inputs may be any that keep to these rules, and one draw needn't show every extreme that they name: `tile_ids`: entry t names the neighbour offset of t // 3 - 1 rows and t % 3 - 1 columns; the 6 entries of one block's list differ from one another, while lists of different blocks, in the same grid row too, may name the same offsets. Only the first tile_counts entries of a block's list are in use.
All inputs are finite; a program needn't handle non-finite values.
Results may differ from the reference program's by a relative error of at most 0.02.
Values may be sent and summed in bfloat16 or wider, within the bound.
No kernel may reach another device: no remote copies, remote signals or barrier semaphores. Data moves between devices by JAX's collectives and lax.ppermute only.
A program may use at most 128 MiB of HBM per device.

```python
import math
import jax
import jax.numpy as jnp
from jax import lax

C = 128
MODES = 64
NY = 1024
OFFSETS = 9
MAXT = 6
BLOCK = 64
NX = 1024
NBLK = 16


def draw_tile_ids(key, part):
    key = jax.random.fold_in(key, 11)
    scores = jax.random.randint(key, (NX, NBLK, OFFSETS), 0, 1 << 20, dtype=jnp.int32)
    scores = scores * 16 + jnp.arange(OFFSETS, dtype=jnp.int32)[None, None, :]
    order = jnp.argsort(scores, axis=-1, stable=True)
    return order[:, :, :MAXT].astype(jnp.int32)


def set_ends(drawn, key, low, high):
    longest = drawn.shape.index(max(drawn.shape))
    spots = []
    for shift in (0, 1):
        where = [jax.random.randint(jax.random.fold_in(key, axis), (), 0, length) for axis, length in enumerate(drawn.shape)]
        where[longest] = (where[longest] + shift) % drawn.shape[longest]
        spots.append(tuple(where))
    return drawn.at[spots[0]].set(low).at[spots[1]].set(high)


def block_scale(key, shape, shards, smallest, high):
    factor_of = 1.0
    for dim, blocks in shards:
        heights = jax.random.uniform(jax.random.fold_in(jax.random.fold_in(key, 6), dim), (blocks,), jnp.float32, smallest / len(shards), high / len(shards))
        factor_of = factor_of * jnp.repeat(jnp.exp(heights), shape[dim] // blocks).reshape((-1,) + (1,) * (len(shape) - 1 - dim))
    return factor_of


def noise(rng, shape, width, limit, pieces=(), held_as=jnp.bfloat16):
    result = width * jax.random.normal(rng, shape, jnp.float32)
    if pieces:
        result = result * block_scale(rng, shape, pieces, -0.22, 0.18)
    return jnp.clip(result, -limit, limit).astype(held_as)


def setup_inputs(seed: int = 0) -> dict:
    seeds = jax.random.split(jax.random.key(seed), 7)
    return {
        "field": noise(seeds[0], (C, NX, NY), 1.0, 6.0, ((0, 4), (1, 128))),
        "cotangent": noise(seeds[1], (C, NX, NY), 1.0, 6.0, ((0, 4), (1, 128))),
        "local_kernel": noise(seeds[2], (OFFSETS, C, C), (OFFSETS * C) ** -0.5, 0.1875, ((1, 4),)),
        "spectral_weight": noise(seeds[3], (2 * MODES, 2 * MODES, C, C), C ** -0.5, 0.5, ((0, 128), (2, 4))),
        "tile_ids": draw_tile_ids(jax.random.fold_in(seeds[6], 71), 0),
        "tile_counts": set_ends(jax.random.randint(seeds[5], (NX, NBLK), 2, MAXT + 1), jax.random.fold_in(seeds[5], 1), 2, MAXT).astype(jnp.int32),
    }


highest = lax.Precision.HIGHEST


def basis_table(length, first, count):
    cells = first + jnp.arange(count, dtype=jnp.int32)
    waves = jnp.arange(MODES, dtype=jnp.int32)
    cos_phase = (cells[:, None] * waves[None, :]) % length
    sin_phase = (cells[:, None] * (waves[None, :] + 1)) % length
    factor = 2.0 * math.pi / length
    scale = (2.0 / length) ** 0.5
    cosines = jnp.cos(cos_phase.astype(jnp.float32) * factor)
    sines = jnp.sin(sin_phase.astype(jnp.float32) * factor)
    return scale * jnp.concatenate([cosines, sines], axis=1)


def tile_masks(tile_ids, tile_counts):
    slots = jnp.arange(tile_ids.shape[-1], dtype=jnp.int32)
    used = (slots[None, None, :] < tile_counts[:, :, None]).astype(jnp.float32)
    labels = jnp.arange(OFFSETS, dtype=jnp.int32)
    hits = (tile_ids[:, :, :, None] == labels[None, None, None, :]).astype(jnp.float32) * used[:, :, :, None]
    block_masks = jnp.transpose(jnp.sum(hits, axis=2), (2, 0, 1))
    row_count = tile_ids.shape[0]
    blocks = tile_ids.shape[1]
    spread = jnp.broadcast_to(block_masks[:, :, :, None], (OFFSETS, row_count, blocks, BLOCK))
    return spread.reshape(OFFSETS, row_count, blocks * BLOCK)


def to_modes(values, table_x, table_y):
    spread = jnp.einsum("cxy,yb->bcx", values.astype(jnp.float32), table_y, precision=highest)
    return jnp.einsum("bcx,xa->bca", spread, table_x, precision=highest).astype(jnp.bfloat16)


def from_modes(coeffs, table_x, table_y):
    rows_part = jnp.einsum("boa,xa->box", coeffs, table_x, precision=highest)
    return jnp.einsum("box,yb->oxy", rows_part, table_y, precision=highest)


def mix_modes(pair):
    weight, modes = pair
    return jnp.einsum("aoi,ia->oa", weight.astype(jnp.float32), modes.astype(jnp.float32), precision=highest)


def back_modes(pair):
    weight, grads = pair
    return jnp.einsum("aoi,oa->ia", weight.astype(jnp.float32), grads.astype(jnp.float32), precision=highest)


def outer_modes(pair):
    grads, modes = pair
    left = jnp.transpose(grads.astype(jnp.float32))
    right = jnp.transpose(modes.astype(jnp.float32))
    return (left[:, :, None] * right[:, None, :]).astype(jnp.bfloat16)


def reference(field, cotangent, local_kernel, spectral_weight, tile_ids, tile_counts):
    table_x = basis_table(NX, 0, NX)
    table_y = basis_table(NY, 0, NY)
    masks = tile_masks(tile_ids, tile_counts)
    flat_field = field.reshape(C, NX * NY)
    local = jnp.zeros((C, NX, NY), jnp.float32)
    for label in range(OFFSETS):
        shift_x = label // 3 - 1
        shift_y = label % 3 - 1
        mixed = jnp.dot(local_kernel[label], flat_field, preferred_element_type=jnp.float32).reshape(C, NX, NY)
        local = local + masks[label] * jnp.roll(mixed, (-shift_x, -shift_y), axis=(1, 2))
    modes = to_modes(field, table_x, table_y)
    mixed_modes = lax.map(mix_modes, (spectral_weight, modes))
    spectral = from_modes(mixed_modes, table_x, table_y)
    pre = local + spectral
    slope = 0.5 * (1.0 + lax.erf(pre * (0.5 ** 0.5))) + pre * jnp.exp(-0.5 * pre * pre) * ((0.5 / math.pi) ** 0.5)
    grad_pre = (cotangent.astype(jnp.float32) * slope).astype(jnp.bfloat16)
    grad_modes = to_modes(grad_pre, table_x, table_y)
    grad_spectral = lax.map(outer_modes, (grad_modes, modes))
    grad_mode_in = lax.map(back_modes, (spectral_weight, grad_modes))
    spectral_back = from_modes(grad_mode_in, table_x, table_y)
    flat_grad = grad_pre.reshape(C, NX * NY)
    local_back = jnp.zeros((C, NX, NY), jnp.float32)
    kernel_rows = []
    for label in range(OFFSETS):
        shift_x = label // 3 - 1
        shift_y = label % 3 - 1
        mixed = jnp.dot(jnp.transpose(local_kernel[label]), flat_grad, preferred_element_type=jnp.float32).reshape(C, NX, NY)
        local_back = local_back + jnp.roll(mixed * masks[label], (shift_x, shift_y), axis=(1, 2))
        masked = (grad_pre.astype(jnp.float32) * masks[label]).astype(jnp.bfloat16).reshape(C, NX * NY)
        moved = jnp.roll(field, (-shift_x, -shift_y), axis=(1, 2)).reshape(C, NX * NY)
        kernel_rows.append(jnp.dot(masked, jnp.transpose(moved), preferred_element_type=jnp.float32))
    grad_kernel = jnp.stack(kernel_rows, axis=0) * ((NX * NY) ** -0.5)
    grad_field = (local_back + spectral_back).astype(jnp.bfloat16)
    return grad_field, grad_spectral, grad_kernel
```

```python
import functools
import math

import jax
import jax.numpy as jnp
import numpy as np
from jax import lax
from jax.experimental import pallas as pl
from jax.experimental.pallas import tpu as pltpu
from jax.sharding import PartitionSpec as P

MODES = 64
NY = 1024
OFFSETS = 9
BLOCK = 64
F32 = jnp.float32
BF16 = jnp.bfloat16


def basis_table(length, count):
    cells = np.arange(count, dtype=np.int64)
    waves = np.arange(MODES, dtype=np.int64)
    factor = 2.0 * math.pi / length
    cosines = np.cos((cells[:, None] * waves[None, :] % length) * factor)
    sines = np.sin((cells[:, None] * (waves[None, :] + 1) % length) * factor)
    return (2.0 / length) ** 0.5 * np.concatenate([cosines, sines], axis=1)


def two_parts(table):
    high = table.astype(jnp.bfloat16)
    low = (table - high.astype(np.float64)).astype(jnp.bfloat16)
    return high, low


def column_table():
    return np.concatenate(two_parts(np.ascontiguousarray(basis_table(NY, NY).T)), axis=0)


def row_table(devices, rows):
    table = basis_table(devices * rows, devices * rows).reshape(devices, rows * 2 * MODES)
    return np.concatenate(two_parts(table), axis=1)


def dot(left, right, left_dim=1, right_dim=0):
    return lax.dot_general(
        left, right, (((left_dim,), (right_dim,)), ((), ())), preferred_element_type=F32
    )


def call(body, outs, *args, scratch=(), flops=10**8):
    single = isinstance(outs, tuple)
    outs = [outs] if single else outs
    shapes = [jax.ShapeDtypeStruct(*o) for o in outs]
    size = sum(math.prod(a.shape) * a.dtype.itemsize for a in list(args) + shapes)
    vmem = pl.BlockSpec(memory_space=pltpu.VMEM)
    result = pl.pallas_call(
        body,
        out_shape=shapes,
        in_specs=[vmem] * len(args),
        out_specs=[vmem] * len(shapes),
        scratch_shapes=list(scratch),
        compiler_params=pltpu.CompilerParams(vmem_limit_bytes=48 * 2**20),
        cost_estimate=pl.CostEstimate(flops=flops, bytes_accessed=size, transcendentals=0),
    )(*args)
    return result[0] if single else result


def column_spread(values, table):
    both = dot(table, values, 1, 1)
    half = both.shape[0] // 2
    return both[:half] + both[half:]


def spread_body(field_ref, table_ref, out_ref):
    out_ref[...] = column_spread(field_ref[...], table_ref[...]).astype(BF16)


def row_modes(moved, table, rows, natural):
    wide = dot(moved, table, 0, 0)
    span = wide.shape[1] // 2
    wide = wide[:, :span] + wide[:, span:]
    waves = span // rows
    count = wide.shape[0] // rows
    if natural:
        cube = wide.reshape(count, rows, span)
        place = lax.broadcasted_iota(jnp.int32, (count, rows, waves), 1)
        total = jnp.zeros((count, rows, waves), F32)
        for x in range(rows):
            total = jnp.where(place == x, cube[:, :, x * waves : (x + 1) * waves], total)
        return jnp.sum(total, axis=1)
    total = jnp.zeros((count, waves), F32)
    for x in range(rows):
        total = total + wide[x * count : (x + 1) * count, x * waves : (x + 1) * waves]
    return total


def modes_body(moved_ref, table_ref, out_ref, *, rows, natural):
    out_ref[...] = row_modes(moved_ref[...], table_ref[...], rows, natural).astype(BF16)


def row_values(coeffs, table, rows, natural):
    count, waves = coeffs.shape
    blocks = []
    if natural:
        spread = jnp.broadcast_to(coeffs[:, None, :], (count, rows, waves))
        place = lax.broadcasted_iota(jnp.int32, (count, rows, waves), 1)
        for x in range(rows):
            blocks.append(
                jnp.where(place == x, spread, 0.0).reshape(count * rows, waves).astype(BF16)
            )
    else:
        low = coeffs.astype(BF16)
        none = jnp.zeros((count, waves), BF16)
        for x in range(rows):
            blocks.append(jnp.concatenate([low if k == x else none for k in range(rows)], axis=0))
    placed = jnp.concatenate(blocks, axis=1)
    span = rows * waves
    return dot(table[:, :span], placed, 1, 1) + dot(table[:, span:], placed, 1, 1)


def mix_body(weight_ref, modes_ref, table_ref, out_ref, *, rows):
    waves = modes_ref.shape[1]
    own = weight_ref.shape[0] // waves
    modes = modes_ref[...]
    lane = lax.broadcasted_iota(jnp.int32, (own, waves), 1)
    step = 8
    total = jnp.zeros((own, waves), F32)
    for first in range(0, waves, step):
        part = dot(weight_ref[first * own : (first + step) * own], modes)
        for k in range(step):
            total = jnp.where(lane == first + k, part[k * own : (k + 1) * own], total)
    out_ref[...] = row_values(total, table_ref[...], rows, False).astype(BF16)


def local_body(kernel_ref, field_ref, low_ref, high_ref, mask_ref, out_ref, acc_ref, *, own):
    rows = field_ref.shape[1]
    channels = kernel_ref.shape[1]
    for j in range(-1, rows + 1):
        ref = low_ref if j < 0 else high_ref if j == rows else field_ref.at[:, j]
        source = ref[...].reshape(channels, NY)
        first = 3 * max(0, j - rows + 2)
        last = 3 * min(3, j + 2)
        product = dot(kernel_ref[first * own : last * own], source)
        for t in range(first, last):
            x = j - (t // 3 - 1)
            term = product[(t - first) * own : (t - first + 1) * own] * mask_ref[
                x * OFFSETS + t : x * OFFSETS + t + 1
            ]
            slot = (x * 3 + t % 3) * own
            if t // 3 == 2:
                acc_ref[slot : slot + own] = acc_ref[slot : slot + own] + term
            elif t // 3 == 1:
                acc_ref[slot : slot + own] = acc_ref[slot : slot + own] + term
            else:
                acc_ref[slot : slot + own] = term
    for x in range(rows):
        slot = x * 3 * own
        out_ref[x * own : (x + 1) * own] = (
            pltpu.roll(acc_ref[slot : slot + own], 1, 1)
            + acc_ref[slot + own : slot + 2 * own]
            + pltpu.roll(acc_ref[slot + 2 * own : slot + 3 * own], NY - 1, 1)
        )


def slope_of(pre):
    return (
        0.5 * (1.0 + lax.erf(pre * 0.5**0.5))
        + pre * jnp.exp(-0.5 * pre * pre) * (0.5 / math.pi) ** 0.5
    )


def grad_body(
    local_ref,
    back_ref,
    cot_ref,
    table_ref,
    field_ref,
    low_ref,
    high_ref,
    mask_ref,
    pre_ref,
    spread_ref,
    kernel_ref,
    *,
    own,
):
    rows = field_ref.shape[1]
    channels = kernel_ref.shape[1]
    back = back_ref[...]
    z = local_ref[...] + dot(jnp.concatenate([back, back], axis=0), table_ref[...], 0, 0)
    grad = cot_ref[...].astype(F32) * slope_of(z)
    grad_low = grad.astype(BF16)
    pre_ref[...] = grad_low
    spread_ref[...] = column_spread(grad_low, table_ref[...]).astype(BF16)
    grad = grad_low.astype(F32)
    shifted = [pltpu.roll(grad, NY - 1, 1), grad, pltpu.roll(grad, 1, 1)]
    total = [jnp.zeros((3 * own, channels), F32) for _ in range(3)]
    for j in range(-1, rows + 1):
        ref = low_ref if j < 0 else high_ref if j == rows else field_ref.at[:, j]
        source = ref[...].reshape(channels, NY)
        for group in range(3):
            x = j - (group - 1)
            if x < 0 or x >= rows:
                continue
            pieces = []
            for k in range(3):
                t = 3 * group + k
                pieces.append(
                    (
                        shifted[k][x * own : (x + 1) * own]
                        * mask_ref[x * OFFSETS + t : x * OFFSETS + t + 1]
                    ).astype(BF16)
                )
            total[group] = total[group] + dot(jnp.concatenate(pieces, axis=0), source, 1, 1)
    for group in range(3):
        kernel_ref[group * 3 * own : (group + 1) * 3 * own] = total[group]


def back_mix_body(moved_ref, table_ref, weight_ref, modes_ref, out_ref, *, rows):
    grads = row_modes(moved_ref[...], table_ref[...], rows, False).astype(BF16)
    modes_ref[...] = grads
    own, waves = grads.shape
    turned = grads.astype(F32).T
    repeat = waves // own
    wide = jnp.concatenate([turned] * repeat, axis=1)
    lane = lax.broadcasted_iota(jnp.int32, (waves, waves), 1) // own
    row = lax.broadcasted_iota(jnp.int32, (waves, waves), 0)
    total = jnp.zeros((waves, weight_ref.shape[1]), F32)
    step = 2
    for first in range(0, own, step):
        placed = [
            jnp.where(row == repeat * (first + k) + lane, wide, 0.0).astype(BF16)
            for k in range(step)
        ]
        total = total + dot(
            jnp.concatenate(placed, axis=1),
            weight_ref[first * waves : (first + step) * waves],
        )
    out_ref[...] = total.T.astype(BF16)


def back_rows_body(parts_ref, table_ref, out_ref, *, rows):
    parts = parts_ref[...].astype(F32)
    total = parts[0]
    for k in range(1, parts.shape[0]):
        total = total + parts[k]
    out_ref[...] = row_values(total, table_ref[...], rows, True).astype(BF16)


def local_back_body(kernel_ref, grad_ref, mask_ref, out_ref, low_ref, high_ref, acc_ref, *, own):
    rows = grad_ref.shape[1]
    channels = kernel_ref.shape[1]
    for x in range(rows):
        product = dot(kernel_ref[...], grad_ref[:, x].reshape(channels, NY))
        for t in range(OFFSETS):
            term = product[t * own : (t + 1) * own] * mask_ref[x * OFFSETS + t : x * OFFSETS + t + 1]
            target = x + t // 3
            slot = (target * 3 + t % 3) * own
            if t // 3 == 2 or x == 0:
                acc_ref[slot : slot + own] = term
            else:
                acc_ref[slot : slot + own] = acc_ref[slot : slot + own] + term
    for target in range(rows + 2):
        slot = target * 3 * own
        value = (
            pltpu.roll(acc_ref[slot : slot + own], NY - 1, 1)
            + acc_ref[slot + own : slot + 2 * own]
            + pltpu.roll(acc_ref[slot + 2 * own : slot + 3 * own], 1, 1)
        )
        if target == 0:
            low_ref[...] = value.astype(BF16)
        elif target == rows + 1:
            high_ref[...] = value.astype(BF16)
        else:
            out_ref[(target - 1) * own : target * own] = value


def final_body(back_ref, table_ref, local_ref, out_ref):
    back = back_ref[...]
    spectral = dot(jnp.concatenate([back, back], axis=0), table_ref[...], 0, 0)
    out_ref[...] = (spectral + local_ref[...]).astype(BF16)


def tile_masks(tile_ids, tile_counts):
    slots = jnp.arange(tile_ids.shape[-1], dtype=jnp.int32)
    used = slots[None, None, :] < tile_counts[:, :, None]
    labels = jnp.arange(OFFSETS, dtype=jnp.int32)
    hits = (tile_ids[:, None, :, :] == labels[None, :, None, None]) & used[:, None]
    return jnp.any(hits, axis=3).astype(BF16)


def spread_tables(blocks):
    cells = np.arange(NY)
    plain = (cells[None, :] // BLOCK == np.arange(blocks)[:, None]).astype(np.float32)
    moved = np.stack([np.roll(plain, k - 1, axis=1) for k in range(3)])
    return plain.astype(jnp.bfloat16), moved.astype(jnp.bfloat16)


def on_device(field, cotangent, local_kernel, spectral_weight, tile_ids, tile_counts):
    own, rows = field.shape[:2]
    devices = lax.axis_size("rows")
    groups = lax.axis_size("chan")
    channels = own * groups
    waves = 2 * MODES
    cells = own * rows
    table_y = jnp.asarray(column_table())
    table_x = jnp.asarray(row_table(devices, rows))
    forward = [(i, (i + 1) % devices) for i in range(devices)]
    backward = [(i, (i - 1) % devices) for i in range(devices)]
    lines = cells // 128

    def exchange(values):
        return lax.all_to_all(values, "rows", split_axis=0, concat_axis=0, tiled=True)

    weight = spectral_weight.reshape(waves * own, channels)
    field_rows = jnp.transpose(field, (1, 0, 2))
    inputs = lax.all_gather(field_rows, "chan")
    spread = call(
        spread_body, ((devices, cells), BF16), field.reshape(cells, NY), table_y
    ).reshape(devices, lines, 128)
    moved = exchange(spread).reshape(devices, cells)

    plain, turned = spread_tables(tile_ids.shape[1])
    small = tile_masks(tile_ids, tile_counts)
    masks = jnp.einsum("xtb,by->xty", small, plain, preferred_element_type=F32)
    masks = masks.reshape(rows * OFFSETS, NY)
    moved_masks = jnp.einsum(
        "xgkb,kby->xgky", small.reshape(rows, 3, 3, -1), turned, preferred_element_type=F32
    ).reshape(rows * OFFSETS, NY)
    pieces = jnp.transpose(local_kernel.reshape(OFFSETS, own, groups, own), (2, 0, 1, 3))
    kernel_lines = OFFSETS * own * own // 128
    cot_rows = jnp.transpose(cotangent, (1, 0, 2)).reshape(cells, NY)

    modes = call(
        functools.partial(modes_body, rows=rows, natural=True), ((own, waves), BF16), moved, table_x
    )
    sent = jnp.concatenate(
        [
            jnp.broadcast_to(modes[None], (groups, own, waves)),
            pieces.reshape(groups, kernel_lines, 128),
        ],
        axis=1,
    )
    got = lax.all_to_all(sent, "chan", split_axis=0, concat_axis=0, tiled=True)
    all_modes = got[:, :own].reshape(channels, waves)
    kernel_back = (
        jnp.transpose(got[:, own:].reshape(groups, OFFSETS, own, own), (1, 3, 0, 2))
    ).reshape(OFFSETS * own, channels)

    rows_part = call(
        functools.partial(mix_body, rows=rows),
        ((devices, cells), BF16),
        weight,
        all_modes,
        table_x,
    ).reshape(devices, lines, 128)
    back = exchange(rows_part).reshape(devices, cells)

    low = lax.ppermute(inputs[:, rows - 1], "rows", forward)
    high = lax.ppermute(inputs[:, 0], "rows", backward)
    local = call(
        functools.partial(local_body, own=own),
        ((cells, NY), F32),
        local_kernel.reshape(OFFSETS * own, channels),
        inputs,
        low,
        high,
        moved_masks,
        scratch=[pltpu.VMEM((rows * 3 * own, NY), F32)],
        flops=10**9,
    )
    grad_pre, grad_spread, kernel_part = call(
        functools.partial(grad_body, own=own),
        [((cells, NY), BF16), ((devices, cells), BF16), ((OFFSETS * own, channels), F32)],
        local,
        back,
        cot_rows,
        table_y,
        inputs,
        low,
        high,
        moved_masks,
        flops=2 * 10**9,
    )
    all_grad = lax.all_gather(grad_pre.reshape(rows, own, NY), "chan")

    def with_kernel(values, share):
        high_part = share.astype(BF16)
        low_part = (share - high_part.astype(F32)).astype(BF16)
        return jnp.concatenate([values.reshape(devices, lines, 128), high_part, low_part], axis=1)

    holders = OFFSETS * own // 3
    share = kernel_part.reshape(holders, 3, channels)
    share = jnp.pad(share, ((0, devices - holders), (0, 0), (0, 0)))
    grad_moved = exchange(with_kernel(grad_spread, share))
    grad_modes, partial_in = call(
        functools.partial(back_mix_body, rows=rows),
        [((own, waves), BF16), ((channels, waves), BF16)],
        grad_moved[:, :lines].reshape(devices, cells),
        table_x,
        weight,
    )
    kernel_sum = jnp.sum(grad_moved[:, lines:].astype(F32), axis=0)
    kernel_sum = (kernel_sum[:3] + kernel_sum[3:]) * (devices * rows * NY) ** (-0.5)
    parts_in = lax.all_to_all(
        partial_in.reshape(groups, own, waves), "chan", split_axis=0, concat_axis=0, tiled=True
    )
    back_part = call(
        functools.partial(back_rows_body, rows=rows), ((devices, cells), BF16), parts_in, table_x
    )
    final = exchange(
        with_kernel(back_part, jnp.broadcast_to(kernel_sum[None], (devices, 3, channels)))
    )
    left = jnp.transpose(grad_modes).astype(F32)
    right = jnp.transpose(all_modes).astype(F32)
    grad_spectral = (left[None, :, :, None] * right[None, :, None, :]).astype(BF16)

    local_back, to_low, to_high = call(
        functools.partial(local_back_body, own=own),
        [((cells, NY), F32), ((own, NY), BF16), ((own, NY), BF16)],
        kernel_back,
        all_grad,
        masks,
        scratch=[pltpu.VMEM(((rows + 2) * 3 * own, NY), F32)],
        flops=10**9,
    )
    from_high = lax.ppermute(to_low, "rows", backward)
    from_low = lax.ppermute(to_high, "rows", forward)
    local_back = jnp.transpose(local_back.reshape(rows, own, NY), (1, 0, 2))
    local_back = local_back.at[:, 0].add(from_low.astype(F32))
    local_back = local_back.at[:, rows - 1].add(from_high.astype(F32))
    grad_field = call(
        final_body,
        ((cells, NY), BF16),
        final[:, :lines].reshape(devices, cells),
        table_y,
        local_back.reshape(cells, NY),
    ).reshape(own, rows, NY)
    summed = final[:holders, lines:].astype(F32)
    grad_kernel = (summed[:, :3] + summed[:, 3:]).reshape(OFFSETS, own, channels)
    return (grad_field, grad_spectral, grad_kernel)


def solution(mesh):
    placed = (
        P("chan", "rows", None),
        P("chan", "rows", None),
        P(None, "chan", None),
        P("rows", None, "chan", None),
        P("rows", None, None),
        P("rows", None),
    )
    return jax.shard_map(
        on_device,
        mesh=mesh,
        in_specs=placed,
        out_specs=(P("chan", "rows", None), P("rows", None, "chan", None), P(None, "chan", None)),
        check_vma=False,
    )
```

```python
import functools
import math

import jax
import jax.numpy as jnp
import numpy as np
from jax import lax
from jax.experimental import pallas as pl
from jax.experimental.pallas import tpu as pltpu
from jax.sharding import PartitionSpec as P

MODES = 64
NY = 1024
OFFSETS = 9
BLOCK = 64
F32 = jnp.float32
BF16 = jnp.bfloat16


def basis_table(length, count):
    cells = np.arange(count, dtype=np.int64)
    waves = np.arange(MODES, dtype=np.int64)
    factor = 2.0 * math.pi / length
    cosines = np.cos((cells[:, None] * waves[None, :] % length) * factor)
    sines = np.sin((cells[:, None] * (waves[None, :] + 1) % length) * factor)
    return (2.0 / length) ** 0.5 * np.concatenate([cosines, sines], axis=1)


def two_parts(table):
    high = table.astype(jnp.bfloat16)
    low = (table - high.astype(np.float64)).astype(jnp.bfloat16)
    return high, low


def column_table():
    return np.concatenate(two_parts(np.ascontiguousarray(basis_table(NY, NY).T)), axis=0)


def row_table(devices, rows):
    table = basis_table(devices * rows, devices * rows).reshape(devices, rows * 2 * MODES)
    return np.concatenate(two_parts(table), axis=1)


def dot(left, right, left_dim=1, right_dim=0):
    return lax.dot_general(
        left, right, (((left_dim,), (right_dim,)), ((), ())), preferred_element_type=F32
    )


def call(body, outs, *args, scratch=(), flops=10**8, far=(), limit=48):
    single = isinstance(outs, tuple)
    outs = [outs] if single else outs
    shapes = [jax.ShapeDtypeStruct(*o) for o in outs]
    size = sum(
        math.prod(a.shape) * a.dtype.itemsize
        for k, a in enumerate(list(args) + shapes)
        if k not in far
    )
    result = pl.pallas_call(
        body,
        out_shape=shapes,
        in_specs=[
            pl.BlockSpec(memory_space=pltpu.HBM if k in far else pltpu.VMEM)
            for k in range(len(args))
        ],
        out_specs=[pl.BlockSpec(memory_space=pltpu.VMEM)] * len(shapes),
        scratch_shapes=list(scratch),
        compiler_params=pltpu.CompilerParams(vmem_limit_bytes=limit * 2**20),
        cost_estimate=pl.CostEstimate(flops=flops, bytes_accessed=size, transcendentals=0),
    )(*args)
    return result[0] if single else result


def every(ref, first, count, stride):
    return ref.at[pl.ds(first, count, stride=stride)]


def put_wide(wide_ref, values):
    for k in range(wide_ref.shape[0]):
        wide_ref[k] = values[:, k * 128 : (k + 1) * 128]


def get_wide(wide_ref):
    return jnp.concatenate([wide_ref[k] for k in range(wide_ref.shape[0])], axis=1)


def wide_rows(wide_ref, first, count, stride):
    return [
        wide_ref.at[k, pl.ds(first, count, stride=stride)] for k in range(wide_ref.shape[0])
    ]


def write_lines(line_ref, values, lines):
    count = values.shape[0]
    every(line_ref, 0, count, lines)[...] = values[:, :128]
    every(line_ref, 1, count, lines)[...] = values[:, 128:]


def read_lines(line_ref, count, lines):
    return jnp.concatenate(
        [every(line_ref, k, count, lines)[...].astype(BF16) for k in range(2)], axis=1
    )


def column_spread(values, table):
    both = dot(table, values, 1, 1)
    half = both.shape[0] // 2
    return both[:half] + both[half:]


def spread_body(
    field_ref, table_ref, out_ref, rows_ref, held, held_table, wide, line_ref, sems, *, rows
):
    field_copy = pltpu.make_async_copy(field_ref, held, sems.at[0])
    table_copy = pltpu.make_async_copy(table_ref, held_table, sems.at[1])
    field_copy.start()
    table_copy.start()
    field_copy.wait()
    put_wide(wide, held[...].astype(F32))
    own = rows_ref.shape[1]
    for x in range(rows):
        views = wide_rows(wide, x, own, rows)
        rows_ref[x] = jnp.concatenate([view[...] for view in views], axis=1).astype(BF16)
    table_copy.wait()
    write_lines(line_ref, column_spread(held[...], held_table[...]), 2)
    out_ref[...] = line_ref[...].astype(BF16)


def row_modes(moved, table, rows, natural):
    wide = dot(moved, table, 0, 0)
    span = wide.shape[1] // 2
    wide = wide[:, :span] + wide[:, span:]
    waves = span // rows
    count = wide.shape[0] // rows
    if natural:
        cube = wide.reshape(count, rows, span)
        place = lax.broadcasted_iota(jnp.int32, (count, rows, waves), 1)
        total = jnp.zeros((count, rows, waves), F32)
        for x in range(rows):
            total = jnp.where(place == x, cube[:, :, x * waves : (x + 1) * waves], total)
        return jnp.sum(total, axis=1)
    total = jnp.zeros((count, waves), F32)
    for x in range(rows):
        total = total + wide[x * count : (x + 1) * count, x * waves : (x + 1) * waves]
    return total


def modes_body(moved_ref, table_ref, piece_ref, ready_ref, out_ref, line_ref, *, rows):
    line_ref[...] = moved_ref[...].astype(F32)
    modes = row_modes(read_lines(line_ref, table_ref.shape[0], 2), table_ref[...], rows, True)
    own = modes.shape[0]
    for k in range(out_ref.shape[0]):
        out_ref[k, :own] = modes.astype(BF16)
        out_ref[k, own:] = piece_ref[k]


def row_values(coeffs, table, rows, natural):
    count, waves = coeffs.shape
    blocks = []
    if natural:
        spread = jnp.broadcast_to(coeffs[:, None, :], (count, rows, waves))
        place = lax.broadcasted_iota(jnp.int32, (count, rows, waves), 1)
        for x in range(rows):
            blocks.append(
                jnp.where(place == x, spread, 0.0).reshape(count * rows, waves).astype(BF16)
            )
    else:
        low = coeffs.astype(BF16)
        none = jnp.zeros((count, waves), BF16)
        for x in range(rows):
            blocks.append(jnp.concatenate([low if k == x else none for k in range(rows)], axis=0))
    placed = jnp.concatenate(blocks, axis=1)
    span = rows * waves
    return dot(table[:, :span], placed, 1, 1) + dot(table[:, span:], placed, 1, 1)


def mix_body(weight_ref, got_ref, table_ref, plain_ref, turned_ref, out_ref, line_ref, *, rows):
    waves = got_ref.shape[2]
    own = weight_ref.shape[0] // waves
    modes = got_ref[:, :own].reshape(got_ref.shape[0] * own, waves)
    lane = lax.broadcasted_iota(jnp.int32, (own, waves), 1)
    step = 8
    total = jnp.zeros((own, waves), F32)
    for first in range(0, waves, step):
        part = dot(weight_ref[first * own : (first + step) * own], modes)
        for k in range(step):
            total = jnp.where(lane == first + k, part[k * own : (k + 1) * own], total)
    line_ref[...] = jnp.zeros(line_ref.shape, F32)
    write_lines(line_ref, row_values(total, table_ref[...], rows, False), 8)
    out_ref[...] = line_ref[...].astype(BF16)


def edges_body(field_ref, after_ref, low_ref, high_ref, sems):
    rows = field_ref.shape[1]
    copies = [
        pltpu.make_async_copy(field_ref.at[:, rows - 1], low_ref, sems.at[0]),
        pltpu.make_async_copy(field_ref.at[:, 0], high_ref, sems.at[1]),
    ]
    for copy in copies:
        copy.start()
    for copy in copies:
        copy.wait()


def local_body(kernel_ref, field_ref, mask_ref, out_ref, acc_ref, *, own):
    rows = field_ref.shape[1]
    channels = kernel_ref.shape[1]
    for j in range(rows):
        source = field_ref[:, j].reshape(channels, NY)
        first = 3 * max(0, j - rows + 2)
        last = 3 * min(3, j + 2)
        product = dot(kernel_ref[first * own : last * own], source)
        for t in range(first, last):
            x = j - (t // 3 - 1)
            term = product[(t - first) * own : (t - first + 1) * own] * mask_ref[
                x * OFFSETS + t : x * OFFSETS + t + 1
            ]
            slot = (x * 3 + t % 3) * own
            if t // 3 == 0 or j == 0:
                acc_ref[slot : slot + own] = term
            else:
                acc_ref[slot : slot + own] = acc_ref[slot : slot + own] + term
    for x in range(rows):
        slot = x * 3 * own
        out_ref[x * own : (x + 1) * own] = turn_back(
            [acc_ref[slot + k * own : slot + (k + 1) * own] for k in range(3)]
        )


def turn_back(parts):
    return pltpu.roll(parts[0], 1, 1) + parts[1] + pltpu.roll(parts[2], NY - 1, 1)


def slope_of(pre):
    return (
        0.5 * (1.0 + lax.erf(pre * 0.5**0.5))
        + pre * jnp.exp(-0.5 * pre * pre) * (0.5 / math.pi) ** 0.5
    )


def write_shares(line_ref, shares, lines, holders, devices):
    for k, share in enumerate(shares):
        high = share.astype(BF16).astype(F32)
        for line, value in ((2 + k, high), (5 + k, share - high)):
            every(line_ref, line, holders, lines)[...] = value
            if holders < devices:
                every(line_ref, holders * lines + line, devices - holders, lines)[...] = jnp.zeros(
                    (devices - holders, value.shape[1]), F32
                )


def grad_body(
    local_ref,
    back_ref,
    cot_ref,
    table_ref,
    field_ref,
    low_ref,
    high_ref,
    mask_ref,
    kernel_ref,
    pre_ref,
    out_ref,
    z_ref,
    back_lines,
    share_ref,
    line_ref,
    *,
    own,
    devices,
):
    rows = field_ref.shape[1]
    channels = kernel_ref.shape[1]
    back_lines[...] = back_ref[...].astype(F32)
    back = read_lines(back_lines, devices, 8)
    z_ref[...] = local_ref[...] + dot(
        jnp.concatenate([back, back], axis=0), table_ref[...], 0, 0
    )
    for x, first, ref in ((0, 0, low_ref), (rows - 1, 6, high_ref)):
        product = dot(
            kernel_ref[first * own : (first + 3) * own], ref[...].reshape(channels, NY)
        )
        parts = [
            product[k * own : (k + 1) * own]
            * mask_ref[x * OFFSETS + first + k : x * OFFSETS + first + k + 1]
            for k in range(3)
        ]
        z_ref[x * own : (x + 1) * own] = z_ref[x * own : (x + 1) * own] + turn_back(parts)
    grad = cot_ref[...].astype(F32) * slope_of(z_ref[...])
    grad_low = grad.astype(BF16)
    pre_ref[...] = grad_low
    write_lines(line_ref, column_spread(grad_low, table_ref[...]), 8)
    grad = grad_low.astype(F32)
    shifted = [pltpu.roll(grad, NY - 1, 1), grad, pltpu.roll(grad, 1, 1)]
    total = [jnp.zeros((3 * own, channels), F32) for _ in range(3)]
    for j in range(-1, rows + 1):
        ref = low_ref if j < 0 else high_ref if j == rows else field_ref.at[:, j]
        source = ref[...].reshape(channels, NY)
        for group in range(3):
            x = j - (group - 1)
            if x < 0 or x >= rows:
                continue
            pieces = []
            for k in range(3):
                t = 3 * group + k
                pieces.append(
                    (
                        shifted[k][x * own : (x + 1) * own]
                        * mask_ref[x * OFFSETS + t : x * OFFSETS + t + 1]
                    ).astype(BF16)
                )
            total[group] = total[group] + dot(jnp.concatenate(pieces, axis=0), source, 1, 1)
    for group in range(3):
        share_ref[group * 3 * own : (group + 1) * 3 * own] = total[group]
    holders = 3 * own
    write_shares(
        line_ref, [every(share_ref, k, holders, 3)[...] for k in range(3)], 8, holders, devices
    )
    out_ref[...] = line_ref[...].astype(BF16)


def back_mix_body(
    moved_ref, table_ref, weight_ref, modes_ref, out_ref, sum_ref, line_ref, *, rows, scale
):
    devices = table_ref.shape[0]
    line_ref[...] = moved_ref[...].astype(F32)
    grads = row_modes(read_lines(line_ref, devices, 8), table_ref[...], rows, False).astype(BF16)
    modes_ref[...] = grads
    own, waves = grads.shape
    turned = grads.astype(F32).T
    repeat = waves // own
    wide = jnp.concatenate([turned] * repeat, axis=1)
    lane = lax.broadcasted_iota(jnp.int32, (waves, waves), 1) // own
    row = lax.broadcasted_iota(jnp.int32, (waves, waves), 0)
    total = jnp.zeros((waves, weight_ref.shape[1]), F32)
    step = 2
    for first in range(0, own, step):
        placed = [
            jnp.where(row == repeat * (first + k) + lane, wide, 0.0).astype(BF16)
            for k in range(step)
        ]
        total = total + dot(
            jnp.concatenate(placed, axis=1),
            weight_ref[first * waves : (first + step) * waves],
        )
    out_ref[...] = total.T.astype(BF16)
    sums = line_ref[0:8]
    for r in range(1, devices):
        sums = sums + line_ref[r * 8 : (r + 1) * 8]
    sum_ref[...] = sums * scale


def back_rows_body(parts_ref, table_ref, sum_ref, *refs, rows):
    out_ref, line_ref = refs[-2:]
    parts = parts_ref[...].astype(F32)
    total = parts[0]
    for k in range(1, parts.shape[0]):
        total = total + parts[k]
    devices = table_ref.shape[0]
    write_lines(line_ref, row_values(total, table_ref[...], rows, True), 8)
    shares = [
        jnp.broadcast_to(
            sum_ref[2 + k : 3 + k] + sum_ref[5 + k : 6 + k], (devices, sum_ref.shape[1])
        )
        for k in range(3)
    ]
    write_shares(line_ref, shares, 8, devices, devices)
    out_ref[...] = line_ref[...].astype(BF16)


def edge_back_body(kernel_ref, grad_ref, mask_ref, low_ref, high_ref, *, own):
    rows = grad_ref.shape[1]
    channels = kernel_ref.shape[1]
    for x, first, ref in ((0, 0, low_ref), (rows - 1, 6, high_ref)):
        product = dot(
            kernel_ref[first * own : (first + 3) * own], grad_ref[:, x].reshape(channels, NY)
        )
        parts = [
            product[k * own : (k + 1) * own]
            * mask_ref[x * OFFSETS + first + k : x * OFFSETS + first + k + 1]
            for k in (2, 1, 0)
        ]
        ref[...] = turn_back(parts).astype(BF16)


def local_back_body(kernel_ref, grad_ref, mask_ref, out_ref, acc_ref, *, own):
    rows = grad_ref.shape[1]
    channels = kernel_ref.shape[1]
    for x in range(rows):
        first = 3 if x == 0 else 0
        last = 6 if x == rows - 1 else 9
        product = dot(
            kernel_ref[first * own : last * own], grad_ref[:, x].reshape(channels, NY)
        )
        for t in range(first, last):
            term = product[(t - first) * own : (t - first + 1) * own] * mask_ref[
                x * OFFSETS + t : x * OFFSETS + t + 1
            ]
            slot = ((x + t // 3 - 1) * 3 + t % 3) * own
            if t // 3 == 2 or (x == 0 and t // 3 == 1):
                acc_ref[slot : slot + own] = term
            else:
                acc_ref[slot : slot + own] = acc_ref[slot : slot + own] + term
    for target in range(rows):
        slot = target * 3 * own
        value = turn_back(
            [acc_ref[slot + k * own : slot + (k + 1) * own] for k in (2, 1, 0)]
        )
        for k, view in enumerate(wide_rows(out_ref, target, own, rows)):
            view[...] = value[:, k * 128 : (k + 1) * 128]


def final_body(
    moved_ref, table_ref, local_ref, low_ref, high_ref, out_ref, share_ref, line_ref, sum_ref
):
    own = low_ref.shape[0]
    rows = local_ref.shape[1] // own
    devices = table_ref.shape[0] // 2
    holders = share_ref.shape[0] // 3
    line_ref[...] = moved_ref[...].astype(F32)
    back = read_lines(line_ref, devices, 8)
    for x, ref in ((0, low_ref), (rows - 1, high_ref)):
        edge = ref[...].astype(F32)
        for k, view in enumerate(wide_rows(sum_ref, x, own, rows)):
            view[...] = edge[:, k * 128 : (k + 1) * 128]
    for x in range(1, rows - 1):
        for view in wide_rows(sum_ref, x, own, rows):
            view[...] = jnp.zeros((own, 128), F32)
    spectral = dot(jnp.concatenate([back, back], axis=0), table_ref[...], 0, 0)
    out_ref[...] = (spectral + get_wide(local_ref) + get_wide(sum_ref)).astype(BF16)
    for k in range(3):
        every(share_ref, k, holders, 3)[...] = (
            every(line_ref, 2 + k, holders, 8)[...] + every(line_ref, 5 + k, holders, 8)[...]
        )


def tile_masks(tile_ids, tile_counts):
    slots = jnp.arange(tile_ids.shape[-1], dtype=jnp.int32)
    used = slots[None, None, :] < tile_counts[:, :, None]
    labels = jnp.arange(OFFSETS, dtype=jnp.int32)
    hits = (tile_ids[:, None, :, :] == labels[None, :, None, None]) & used[:, None]
    return jnp.any(hits, axis=3).astype(BF16)


def spread_tables(blocks):
    cells = np.arange(NY)
    plain = (cells[None, :] // BLOCK == np.arange(blocks)[:, None]).astype(np.float32)
    moved = np.stack([np.roll(plain, k - 1, axis=1) for k in range(3)])
    return plain.astype(jnp.bfloat16), moved.astype(jnp.bfloat16)


def on_device(field, cotangent, local_kernel, spectral_weight, tile_ids, tile_counts):
    own, rows = field.shape[:2]
    devices = lax.axis_size("rows")
    groups = lax.axis_size("chan")
    channels = own * groups
    waves = 2 * MODES
    cells = own * rows
    table_y = jnp.asarray(column_table())
    table_x = jnp.asarray(row_table(devices, rows))
    forward = [(i, (i + 1) % devices) for i in range(devices)]
    backward = [(i, (i - 1) % devices) for i in range(devices)]
    def exchange(lines):
        cube = lines.reshape(devices, -1, 128)
        moved = lax.all_to_all(cube, "rows", split_axis=0, concat_axis=0, tiled=True)
        return moved.reshape(lines.shape)

    def swap(values):
        return lax.all_to_all(values, "chan", split_axis=0, concat_axis=0, tiled=True)

    weight = spectral_weight.reshape(waves * own, channels)
    two = pltpu.VMEM((2 * devices, 128), F32)
    eight = pltpu.VMEM((8 * devices, 128), F32)
    wide = pltpu.VMEM((NY // 128, cells, 128), F32)
    spread, field_rows = call(
        functools.partial(spread_body, rows=rows),
        [((2 * devices, 128), BF16), ((rows, own, NY), BF16)],
        field.reshape(cells, NY),
        table_y,
        far=(0, 1),
        limit=61,
        scratch=[
            pltpu.VMEM((cells, NY), BF16),
            pltpu.VMEM(table_y.shape, BF16),
            wide,
            two,
            pltpu.SemaphoreType.DMA((2,)),
        ],
    )
    inputs = lax.all_gather(field_rows, "chan")
    moved = exchange(spread)

    pieces = jnp.transpose(local_kernel.reshape(OFFSETS, own, groups, own), (2, 0, 1, 3))
    pieces = pieces.reshape(groups, OFFSETS * own * own // 128, 128)
    kernel_lines = pieces.shape[1]
    pieces = jnp.pad(pieces, ((0, 0), (0, -kernel_lines % 16), (0, 0)))
    cot_rows = jnp.transpose(cotangent, (1, 0, 2)).reshape(cells, NY)
    plain, turned = spread_tables(tile_ids.shape[1])
    small = tile_masks(tile_ids, tile_counts)
    masks = jnp.einsum("xtb,by->xty", small, plain, preferred_element_type=F32)
    masks = masks.reshape(rows * OFFSETS, NY)
    moved_masks = jnp.einsum(
        "xgkb,kby->xgky", small.reshape(rows, 3, 3, -1), turned, preferred_element_type=F32
    ).reshape(rows * OFFSETS, NY)

    sent = call(
        functools.partial(modes_body, rows=rows),
        ((groups, own + pieces.shape[1], waves), BF16),
        moved,
        table_x,
        pieces,
        cot_rows,
        far=(3,),
        scratch=[two],
    )
    got = swap(sent)
    rows_part = call(
        functools.partial(mix_body, rows=rows),
        ((8 * devices, 128), BF16),
        weight,
        got,
        table_x,
        masks,
        moved_masks,
        far=(3, 4),
        scratch=[pltpu.VMEM((8 * devices, 128), F32)],
    )
    back = exchange(rows_part)
    low, high = call(
        edges_body,
        [((groups, own, NY), BF16)] * 2,
        inputs,
        rows_part,
        far=(0, 1),
        scratch=[pltpu.SemaphoreType.DMA((2,))],
    )
    low = lax.ppermute(low, "rows", forward)
    high = lax.ppermute(high, "rows", backward)
    kernel_rows = local_kernel.reshape(OFFSETS * own, channels)
    local = call(
        functools.partial(local_body, own=own),
        ((cells, NY), F32),
        kernel_rows,
        inputs,
        moved_masks,
        scratch=[pltpu.VMEM((rows * 3 * own, NY), F32)],
        flops=10**9,
    )
    grad_pre, grad_spread = call(
        functools.partial(grad_body, own=own, devices=devices),
        [((cells, NY), BF16), ((8 * devices, 128), BF16)],
        local,
        back,
        cot_rows,
        table_y,
        inputs,
        low,
        high,
        moved_masks,
        kernel_rows,
        scratch=[
            pltpu.VMEM((cells, NY), F32),
            pltpu.VMEM((8 * devices, 128), F32),
            pltpu.VMEM((OFFSETS * own, channels), F32),
            eight,
        ],
        flops=2 * 10**9,
    )
    all_grad = lax.all_gather(grad_pre.reshape(rows, own, NY), "chan")
    grad_moved = exchange(grad_spread)
    grad_modes, partial_in, kernel_sum = call(
        functools.partial(back_mix_body, rows=rows, scale=(devices * rows * NY) ** (-0.5)),
        [((own, waves), BF16), ((channels, waves), BF16), ((8, channels), F32)],
        grad_moved,
        table_x,
        weight,
        scratch=[eight],
    )
    parts_in = swap(partial_in.reshape(groups, own, waves))
    all_modes = got[:, :own].reshape(channels, waves)
    kernel_back = (
        jnp.transpose(
            got[:, own : own + kernel_lines].reshape(groups, OFFSETS, own, own), (1, 3, 0, 2)
        )
    ).reshape(OFFSETS * own, channels)
    left = jnp.transpose(grad_modes).astype(F32)
    right = jnp.transpose(all_modes).astype(F32)
    grad_spectral = (left[None, :, :, None] * right[None, :, None, :]).astype(BF16)
    back_part = call(
        functools.partial(back_rows_body, rows=rows),
        ((8 * devices, 128), BF16),
        parts_in,
        table_x,
        kernel_sum,
        all_grad[0, 0, :16, :128],
        grad_spectral,
        kernel_back,
        far=(4, 5),
        scratch=[eight],
    )
    final = exchange(back_part)
    to_low, to_high = call(
        functools.partial(edge_back_body, own=own),
        [((own, NY), BF16), ((own, NY), BF16)],
        kernel_back,
        all_grad,
        masks,
    )
    from_high = lax.ppermute(to_low, "rows", backward)
    from_low = lax.ppermute(to_high, "rows", forward)
    local_back = call(
        functools.partial(local_back_body, own=own),
        ((NY // 128, cells, 128), F32),
        kernel_back,
        all_grad,
        masks,
        scratch=[pltpu.VMEM((rows * 3 * own, NY), F32)],
        flops=10**9,
    )
    grad_field, grad_kernel = call(
        final_body,
        [((cells, NY), BF16), ((OFFSETS * own, channels), F32)],
        final,
        table_y,
        local_back,
        from_low,
        from_high,
        scratch=[eight, wide],
    )
    return (
        grad_field.reshape(own, rows, NY),
        grad_spectral,
        grad_kernel.reshape(OFFSETS, own, channels),
    )


def solution(mesh):
    placed = (
        P("chan", "rows", None),
        P("chan", "rows", None),
        P(None, "chan", None),
        P("rows", None, "chan", None),
        P("rows", None, None),
        P("rows", None),
    )
    return jax.shard_map(
        on_device,
        mesh=mesh,
        in_specs=placed,
        out_specs=(P("chan", "rows", None), P("rows", None, "chan", None), P(None, "chan", None)),
        check_vma=False,
    )
```

```python
import functools
import math

import jax
import jax.numpy as jnp
import numpy as np
from jax import lax
from jax.experimental import pallas as pl
from jax.experimental.pallas import tpu as pltpu
from jax.sharding import PartitionSpec as P

MODES = 64
NY = 1024
OFFSETS = 9
BLOCK = 64
F32 = jnp.float32
BF16 = jnp.bfloat16


def basis_table(length, count):
    cells = np.arange(count, dtype=np.int64)
    waves = np.arange(MODES, dtype=np.int64)
    factor = 2.0 * math.pi / length
    cosines = np.cos((cells[:, None] * waves[None, :] % length) * factor)
    sines = np.sin((cells[:, None] * (waves[None, :] + 1) % length) * factor)
    return (2.0 / length) ** 0.5 * np.concatenate([cosines, sines], axis=1)


def two_parts(table):
    high = table.astype(jnp.bfloat16)
    low = (table - high.astype(np.float64)).astype(jnp.bfloat16)
    return high, low


def column_table():
    return np.concatenate(two_parts(np.ascontiguousarray(basis_table(NY, NY).T)), axis=0)


def row_table(devices, rows):
    table = basis_table(devices * rows, devices * rows).reshape(devices, rows * 2 * MODES)
    return np.concatenate(two_parts(table), axis=1)


def dot(left, right, left_dim=1, right_dim=0):
    return lax.dot_general(
        left, right, (((left_dim,), (right_dim,)), ((), ())), preferred_element_type=F32
    )


def call(body, outs, *args, scratch=(), flops=10**8, far=(), limit=48):
    single = isinstance(outs, tuple)
    outs = [outs] if single else outs
    shapes = [jax.ShapeDtypeStruct(*o) for o in outs]
    size = sum(
        math.prod(a.shape) * a.dtype.itemsize
        for k, a in enumerate(list(args) + shapes)
        if k not in far
    )
    result = pl.pallas_call(
        body,
        out_shape=shapes,
        in_specs=[
            pl.BlockSpec(memory_space=pltpu.HBM if k in far else pltpu.VMEM)
            for k in range(len(args))
        ],
        out_specs=[pl.BlockSpec(memory_space=pltpu.VMEM)] * len(shapes),
        scratch_shapes=list(scratch),
        compiler_params=pltpu.CompilerParams(vmem_limit_bytes=limit * 2**20),
        cost_estimate=pl.CostEstimate(flops=flops, bytes_accessed=size, transcendentals=0),
    )(*args)
    return result[0] if single else result


def every(ref, first, count, stride):
    return ref.at[pl.ds(first, count, stride=stride)]


def put_wide(wide_ref, values):
    for k in range(wide_ref.shape[0]):
        wide_ref[k] = values[:, k * 128 : (k + 1) * 128]


def get_wide(wide_ref):
    return jnp.concatenate([wide_ref[k] for k in range(wide_ref.shape[0])], axis=1)


def wide_rows(wide_ref, first, count, stride):
    return [
        wide_ref.at[k, pl.ds(first, count, stride=stride)] for k in range(wide_ref.shape[0])
    ]


def write_lines(line_ref, values, lines):
    count = values.shape[0]
    every(line_ref, 0, count, lines)[...] = values[:, :128]
    every(line_ref, 1, count, lines)[...] = values[:, 128:]


def read_lines(line_ref, count, lines):
    return jnp.concatenate(
        [every(line_ref, k, count, lines)[...].astype(BF16) for k in range(2)], axis=1
    )


def column_spread(values, table):
    both = dot(table, values, 1, 1)
    half = both.shape[0] // 2
    return both[:half] + both[half:]


def spread_body(
    field_ref, table_ref, out_ref, rows_ref, held, held_table, wide, line_ref, sems, *, rows
):
    field_copy = pltpu.make_async_copy(field_ref, held, sems.at[0])
    table_copy = pltpu.make_async_copy(table_ref, held_table, sems.at[1])
    field_copy.start()
    table_copy.start()
    field_copy.wait()
    put_wide(wide, held[...].astype(F32))
    own = rows_ref.shape[1]
    for x in range(rows):
        views = wide_rows(wide, x, own, rows)
        rows_ref[x] = jnp.concatenate([view[...] for view in views], axis=1).astype(BF16)
    table_copy.wait()
    write_lines(line_ref, column_spread(held[...], held_table[...]), 2)
    out_ref[...] = line_ref[...].astype(BF16)


def row_modes(moved, table, rows, natural):
    wide = dot(moved, table, 0, 0)
    span = wide.shape[1] // 2
    wide = wide[:, :span] + wide[:, span:]
    waves = span // rows
    count = wide.shape[0] // rows
    if natural:
        cube = wide.reshape(count, rows, span)
        place = lax.broadcasted_iota(jnp.int32, (count, rows, waves), 1)
        total = jnp.zeros((count, rows, waves), F32)
        for x in range(rows):
            total = jnp.where(place == x, cube[:, :, x * waves : (x + 1) * waves], total)
        return jnp.sum(total, axis=1)
    total = jnp.zeros((count, waves), F32)
    for x in range(rows):
        total = total + wide[x * count : (x + 1) * count, x * waves : (x + 1) * waves]
    return total


def modes_body(moved_ref, table_ref, piece_ref, ready_ref, out_ref, line_ref, *, rows):
    line_ref[...] = moved_ref[...].astype(F32)
    modes = row_modes(read_lines(line_ref, table_ref.shape[0], 2), table_ref[...], rows, True)
    own = modes.shape[0]
    for k in range(out_ref.shape[0]):
        out_ref[k, :own] = modes.astype(BF16)
        out_ref[k, own:] = piece_ref[k]


def row_values(coeffs, table, rows, natural):
    count, waves = coeffs.shape
    blocks = []
    if natural:
        spread = jnp.broadcast_to(coeffs[:, None, :], (count, rows, waves))
        place = lax.broadcasted_iota(jnp.int32, (count, rows, waves), 1)
        for x in range(rows):
            blocks.append(
                jnp.where(place == x, spread, 0.0).reshape(count * rows, waves).astype(BF16)
            )
    else:
        low = coeffs.astype(BF16)
        none = jnp.zeros((count, waves), BF16)
        for x in range(rows):
            blocks.append(jnp.concatenate([low if k == x else none for k in range(rows)], axis=0))
    placed = jnp.concatenate(blocks, axis=1)
    span = rows * waves
    return dot(table[:, :span], placed, 1, 1) + dot(table[:, span:], placed, 1, 1)


def mix_body(weight_ref, got_ref, table_ref, plain_ref, turned_ref, out_ref, line_ref, *, rows):
    waves = got_ref.shape[2]
    own = weight_ref.shape[0] // waves
    modes = got_ref[:, :own].reshape(got_ref.shape[0] * own, waves)
    lane = lax.broadcasted_iota(jnp.int32, (own, waves), 1)
    step = 8
    total = jnp.zeros((own, waves), F32)
    for first in range(0, waves, step):
        part = dot(weight_ref[first * own : (first + step) * own], modes)
        for k in range(step):
            total = jnp.where(lane == first + k, part[k * own : (k + 1) * own], total)
    write_lines(line_ref, row_values(total, table_ref[...], rows, False), 2)
    out_ref[...] = line_ref[...].astype(BF16)


def edges_body(field_ref, after_ref, low_ref, high_ref, sems):
    rows = field_ref.shape[1]
    copies = [
        pltpu.make_async_copy(field_ref.at[:, rows - 1], low_ref, sems.at[0]),
        pltpu.make_async_copy(field_ref.at[:, 0], high_ref, sems.at[1]),
    ]
    for copy in copies:
        copy.start()
    for copy in copies:
        copy.wait()


def local_body(kernel_ref, field_ref, mask_ref, out_ref, acc_ref, *, own):
    rows = field_ref.shape[1]
    channels = kernel_ref.shape[1]
    for j in range(rows):
        source = field_ref[:, j].reshape(channels, NY)
        first = 3 * max(0, j - rows + 2)
        last = 3 * min(3, j + 2)
        product = dot(kernel_ref[first * own : last * own], source)
        for t in range(first, last):
            x = j - (t // 3 - 1)
            term = product[(t - first) * own : (t - first + 1) * own] * mask_ref[
                x * OFFSETS + t : x * OFFSETS + t + 1
            ]
            slot = (x * 3 + t % 3) * own
            if t // 3 == 0 or j == 0:
                acc_ref[slot : slot + own] = term
            else:
                acc_ref[slot : slot + own] = acc_ref[slot : slot + own] + term
    for x in range(rows):
        slot = x * 3 * own
        out_ref[x * own : (x + 1) * own] = turn_back(
            [acc_ref[slot + k * own : slot + (k + 1) * own] for k in range(3)]
        )


def turn_back(parts):
    return pltpu.roll(parts[0], 1, 1) + parts[1] + pltpu.roll(parts[2], NY - 1, 1)


def slope_of(pre):
    return (
        0.5 * (1.0 + lax.erf(pre * 0.5**0.5))
        + pre * jnp.exp(-0.5 * pre * pre) * (0.5 / math.pi) ** 0.5
    )


def write_shares(line_ref, shares, lines, holders, devices):
    for k, share in enumerate(shares):
        high = share.astype(BF16).astype(F32)
        for line, value in ((2 + k, high), (5 + k, share - high)):
            every(line_ref, line, holders, lines)[...] = value
            if holders < devices:
                every(line_ref, holders * lines + line, devices - holders, lines)[...] = jnp.zeros(
                    (devices - holders, value.shape[1]), F32
                )


def grad_body(
    local_ref,
    back_ref,
    cot_ref,
    table_ref,
    field_ref,
    low_ref,
    high_ref,
    mask_ref,
    kernel_ref,
    pre_ref,
    out_ref,
    z_ref,
    back_lines,
    share_ref,
    line_ref,
    *,
    own,
    devices,
):
    rows = field_ref.shape[1]
    channels = kernel_ref.shape[1]
    back_lines[...] = back_ref[...].astype(F32)
    back = read_lines(back_lines, devices, 2)
    z_ref[...] = local_ref[...] + dot(
        jnp.concatenate([back, back], axis=0), table_ref[...], 0, 0
    )
    for x, first, ref in ((0, 0, low_ref), (rows - 1, 6, high_ref)):
        product = dot(
            kernel_ref[first * own : (first + 3) * own], ref[...].reshape(channels, NY)
        )
        parts = [
            product[k * own : (k + 1) * own]
            * mask_ref[x * OFFSETS + first + k : x * OFFSETS + first + k + 1]
            for k in range(3)
        ]
        z_ref[x * own : (x + 1) * own] = z_ref[x * own : (x + 1) * own] + turn_back(parts)
    grad = cot_ref[...].astype(F32) * slope_of(z_ref[...])
    grad_low = grad.astype(BF16)
    pre_ref[...] = grad_low
    write_lines(line_ref, column_spread(grad_low, table_ref[...]), 8)
    grad = grad_low.astype(F32)
    shifted = [pltpu.roll(grad, NY - 1, 1), grad, pltpu.roll(grad, 1, 1)]
    total = [jnp.zeros((3 * own, channels), F32) for _ in range(3)]
    for j in range(-1, rows + 1):
        ref = low_ref if j < 0 else high_ref if j == rows else field_ref.at[:, j]
        source = ref[...].reshape(channels, NY)
        for group in range(3):
            x = j - (group - 1)
            if x < 0 or x >= rows:
                continue
            pieces = []
            for k in range(3):
                t = 3 * group + k
                pieces.append(
                    (
                        shifted[k][x * own : (x + 1) * own]
                        * mask_ref[x * OFFSETS + t : x * OFFSETS + t + 1]
                    ).astype(BF16)
                )
            total[group] = total[group] + dot(jnp.concatenate(pieces, axis=0), source, 1, 1)
    for group in range(3):
        share_ref[group * 3 * own : (group + 1) * 3 * own] = total[group]
    holders = 3 * own
    write_shares(
        line_ref, [every(share_ref, k, holders, 3)[...] for k in range(3)], 8, holders, devices
    )
    out_ref[...] = line_ref[...].astype(BF16)


def back_mix_body(
    moved_ref, table_ref, weight_ref, modes_ref, out_ref, sum_ref, line_ref, *, rows, scale
):
    devices = table_ref.shape[0]
    line_ref[...] = moved_ref[...].astype(F32)
    grads = row_modes(read_lines(line_ref, devices, 8), table_ref[...], rows, False).astype(BF16)
    modes_ref[...] = grads
    own, waves = grads.shape
    turned = grads.astype(F32).T
    repeat = waves // own
    wide = jnp.concatenate([turned] * repeat, axis=1)
    lane = lax.broadcasted_iota(jnp.int32, (waves, waves), 1) // own
    row = lax.broadcasted_iota(jnp.int32, (waves, waves), 0)
    total = jnp.zeros((waves, weight_ref.shape[1]), F32)
    step = 2
    for first in range(0, own, step):
        placed = [
            jnp.where(row == repeat * (first + k) + lane, wide, 0.0).astype(BF16)
            for k in range(step)
        ]
        total = total + dot(
            jnp.concatenate(placed, axis=1),
            weight_ref[first * waves : (first + step) * waves],
        )
    out_ref[...] = total.T.astype(BF16)
    sums = line_ref[0:8]
    for r in range(1, devices):
        sums = sums + line_ref[r * 8 : (r + 1) * 8]
    sum_ref[...] = sums * scale


def back_rows_body(parts_ref, table_ref, sum_ref, *refs, rows):
    out_ref, line_ref = refs[-2:]
    parts = parts_ref[...].astype(F32)
    total = parts[0]
    for k in range(1, parts.shape[0]):
        total = total + parts[k]
    devices = table_ref.shape[0]
    write_lines(line_ref, row_values(total, table_ref[...], rows, True), 8)
    shares = [
        jnp.broadcast_to(
            sum_ref[2 + k : 3 + k] + sum_ref[5 + k : 6 + k], (devices, sum_ref.shape[1])
        )
        for k in range(3)
    ]
    write_shares(line_ref, shares, 8, devices, devices)
    out_ref[...] = line_ref[...].astype(BF16)


def edge_back_body(kernel_ref, grad_ref, mask_ref, low_ref, high_ref, *, own):
    rows = grad_ref.shape[1]
    channels = kernel_ref.shape[1]
    for x, first, ref in ((0, 0, low_ref), (rows - 1, 6, high_ref)):
        product = dot(
            kernel_ref[first * own : (first + 3) * own], grad_ref[:, x].reshape(channels, NY)
        )
        parts = [
            product[k * own : (k + 1) * own]
            * mask_ref[x * OFFSETS + first + k : x * OFFSETS + first + k + 1]
            for k in (2, 1, 0)
        ]
        ref[...] = turn_back(parts).astype(BF16)


def local_back_body(kernel_ref, grad_ref, mask_ref, out_ref, acc_ref, *, own):
    rows = grad_ref.shape[1]
    channels = kernel_ref.shape[1]
    for x in range(rows):
        first = 3 if x == 0 else 0
        last = 6 if x == rows - 1 else 9
        product = dot(
            kernel_ref[first * own : last * own], grad_ref[:, x].reshape(channels, NY)
        )
        for t in range(first, last):
            term = product[(t - first) * own : (t - first + 1) * own] * mask_ref[
                x * OFFSETS + t : x * OFFSETS + t + 1
            ]
            slot = ((x + t // 3 - 1) * 3 + t % 3) * own
            if t // 3 == 2 or (x == 0 and t // 3 == 1):
                acc_ref[slot : slot + own] = term
            else:
                acc_ref[slot : slot + own] = acc_ref[slot : slot + own] + term
    for target in range(rows):
        slot = target * 3 * own
        value = turn_back(
            [acc_ref[slot + k * own : slot + (k + 1) * own] for k in (2, 1, 0)]
        )
        for k, view in enumerate(wide_rows(out_ref, target, own, rows)):
            view[...] = value[:, k * 128 : (k + 1) * 128]


def final_body(
    moved_ref, table_ref, local_ref, low_ref, high_ref, out_ref, share_ref, line_ref, sum_ref
):
    own = low_ref.shape[0]
    rows = local_ref.shape[1] // own
    devices = table_ref.shape[0] // 2
    holders = share_ref.shape[0] // 3
    line_ref[...] = moved_ref[...].astype(F32)
    back = read_lines(line_ref, devices, 8)
    for x, ref in ((0, low_ref), (rows - 1, high_ref)):
        edge = ref[...].astype(F32)
        for k, view in enumerate(wide_rows(sum_ref, x, own, rows)):
            view[...] = edge[:, k * 128 : (k + 1) * 128]
    for x in range(1, rows - 1):
        for view in wide_rows(sum_ref, x, own, rows):
            view[...] = jnp.zeros((own, 128), F32)
    spectral = dot(jnp.concatenate([back, back], axis=0), table_ref[...], 0, 0)
    out_ref[...] = (spectral + get_wide(local_ref) + get_wide(sum_ref)).astype(BF16)
    for k in range(3):
        every(share_ref, k, holders, 3)[...] = (
            every(line_ref, 2 + k, holders, 8)[...] + every(line_ref, 5 + k, holders, 8)[...]
        )


def tile_masks(tile_ids, tile_counts):
    slots = jnp.arange(tile_ids.shape[-1], dtype=jnp.int32)
    used = slots[None, None, :] < tile_counts[:, :, None]
    labels = jnp.arange(OFFSETS, dtype=jnp.int32)
    hits = (tile_ids[:, None, :, :] == labels[None, :, None, None]) & used[:, None]
    return jnp.any(hits, axis=3).astype(BF16)


def spread_tables(blocks):
    cells = np.arange(NY)
    plain = (cells[None, :] // BLOCK == np.arange(blocks)[:, None]).astype(np.float32)
    moved = np.stack([np.roll(plain, k - 1, axis=1) for k in range(3)])
    return plain.astype(jnp.bfloat16), moved.astype(jnp.bfloat16)


def on_device(field, cotangent, local_kernel, spectral_weight, tile_ids, tile_counts):
    own, rows = field.shape[:2]
    devices = lax.axis_size("rows")
    groups = lax.axis_size("chan")
    channels = own * groups
    waves = 2 * MODES
    cells = own * rows
    table_y = jnp.asarray(column_table())
    table_x = jnp.asarray(row_table(devices, rows))
    forward = [(i, (i + 1) % devices) for i in range(devices)]
    backward = [(i, (i - 1) % devices) for i in range(devices)]
    def exchange(lines):
        cube = lines.reshape(devices, -1, 128)
        moved = lax.all_to_all(cube, "rows", split_axis=0, concat_axis=0, tiled=True)
        return moved.reshape(lines.shape)

    def swap(values):
        return lax.all_to_all(values, "chan", split_axis=0, concat_axis=0, tiled=True)

    weight = spectral_weight.reshape(waves * own, channels)
    two = pltpu.VMEM((2 * devices, 128), F32)
    eight = pltpu.VMEM((8 * devices, 128), F32)
    wide = pltpu.VMEM((NY // 128, cells, 128), F32)
    spread, field_rows = call(
        functools.partial(spread_body, rows=rows),
        [((2 * devices, 128), BF16), ((rows, own, NY), BF16)],
        field.reshape(cells, NY),
        table_y,
        far=(0, 1),
        limit=61,
        scratch=[
            pltpu.VMEM((cells, NY), BF16),
            pltpu.VMEM(table_y.shape, BF16),
            wide,
            two,
            pltpu.SemaphoreType.DMA((2,)),
        ],
    )
    inputs = lax.all_gather(field_rows, "chan")
    moved = exchange(spread)

    pieces = jnp.transpose(local_kernel.reshape(OFFSETS, own, groups, own), (2, 0, 1, 3))
    pieces = pieces.reshape(groups, OFFSETS * own * own // 128, 128)
    kernel_lines = pieces.shape[1]
    pieces = jnp.pad(pieces, ((0, 0), (0, -kernel_lines % 16), (0, 0)))
    cot_rows = jnp.transpose(cotangent, (1, 0, 2)).reshape(cells, NY)
    plain, turned = spread_tables(tile_ids.shape[1])
    small = tile_masks(tile_ids, tile_counts)
    masks = jnp.einsum("xtb,by->xty", small, plain, preferred_element_type=F32)
    masks = masks.reshape(rows * OFFSETS, NY)
    moved_masks = jnp.einsum(
        "xgkb,kby->xgky", small.reshape(rows, 3, 3, -1), turned, preferred_element_type=F32
    ).reshape(rows * OFFSETS, NY)

    sent = call(
        functools.partial(modes_body, rows=rows),
        ((groups, own + pieces.shape[1], waves), BF16),
        moved,
        table_x,
        pieces,
        cot_rows,
        far=(3,),
        scratch=[two],
    )
    got = swap(sent)
    rows_part = call(
        functools.partial(mix_body, rows=rows),
        ((2 * devices, 128), BF16),
        weight,
        got,
        table_x,
        masks,
        moved_masks,
        far=(3, 4),
        scratch=[two],
    )
    back = exchange(rows_part)
    low, high = call(
        edges_body,
        [((groups, own, NY), BF16)] * 2,
        inputs,
        back,
        far=(0, 1),
        scratch=[pltpu.SemaphoreType.DMA((2,))],
    )
    low = lax.ppermute(low, "rows", forward)
    high = lax.ppermute(high, "rows", backward)
    kernel_rows = local_kernel.reshape(OFFSETS * own, channels)
    local = call(
        functools.partial(local_body, own=own),
        ((cells, NY), F32),
        kernel_rows,
        inputs,
        moved_masks,
        scratch=[pltpu.VMEM((rows * 3 * own, NY), F32)],
        flops=10**9,
    )
    grad_pre, grad_spread = call(
        functools.partial(grad_body, own=own, devices=devices),
        [((cells, NY), BF16), ((8 * devices, 128), BF16)],
        local,
        back,
        cot_rows,
        table_y,
        inputs,
        low,
        high,
        moved_masks,
        kernel_rows,
        scratch=[
            pltpu.VMEM((cells, NY), F32),
            two,
            pltpu.VMEM((OFFSETS * own, channels), F32),
            eight,
        ],
        flops=2 * 10**9,
    )
    all_grad = lax.all_gather(grad_pre.reshape(rows, own, NY), "chan")
    grad_moved = exchange(grad_spread)
    grad_modes, partial_in, kernel_sum = call(
        functools.partial(back_mix_body, rows=rows, scale=(devices * rows * NY) ** (-0.5)),
        [((own, waves), BF16), ((channels, waves), BF16), ((8, channels), F32)],
        grad_moved,
        table_x,
        weight,
        scratch=[eight],
    )
    parts_in = swap(partial_in.reshape(groups, own, waves))
    all_modes = got[:, :own].reshape(channels, waves)
    kernel_back = (
        jnp.transpose(
            got[:, own : own + kernel_lines].reshape(groups, OFFSETS, own, own), (1, 3, 0, 2)
        )
    ).reshape(OFFSETS * own, channels)
    left = jnp.transpose(grad_modes).astype(F32)
    right = jnp.transpose(all_modes).astype(F32)
    grad_spectral = (left[None, :, :, None] * right[None, :, None, :]).astype(BF16)
    back_part = call(
        functools.partial(back_rows_body, rows=rows),
        ((8 * devices, 128), BF16),
        parts_in,
        table_x,
        kernel_sum,
        grad_spectral,
        kernel_back,
        far=(3, 4),
        scratch=[eight],
    )
    final = exchange(back_part)
    to_low, to_high = call(
        functools.partial(edge_back_body, own=own),
        [((own, NY), BF16), ((own, NY), BF16)],
        kernel_back,
        all_grad,
        masks,
        flops=10**8,
    )
    from_high = lax.ppermute(to_low, "rows", backward)
    from_low = lax.ppermute(to_high, "rows", forward)
    local_back = call(
        functools.partial(local_back_body, own=own),
        ((NY // 128, cells, 128), F32),
        kernel_back,
        all_grad,
        masks,
        scratch=[pltpu.VMEM((rows * 3 * own, NY), F32)],
        flops=10**9,
    )
    grad_field, grad_kernel = call(
        final_body,
        [((cells, NY), BF16), ((OFFSETS * own, channels), F32)],
        final,
        table_y,
        local_back,
        from_low,
        from_high,
        scratch=[eight, wide],
    )
    return (
        grad_field.reshape(own, rows, NY),
        grad_spectral,
        grad_kernel.reshape(OFFSETS, own, channels),
    )


def solution(mesh):
    placed = (
        P("chan", "rows", None),
        P("chan", "rows", None),
        P(None, "chan", None),
        P("rows", None, "chan", None),
        P("rows", None, None),
        P("rows", None),
    )
    return jax.shard_map(
        on_device,
        mesh=mesh,
        in_specs=placed,
        out_specs=(P("chan", "rows", None), P("rows", None, "chan", None), P(None, "chan", None)),
        check_vma=False,
    )
```

```python
import functools
import math

import jax
import jax.numpy as jnp
import numpy as np
from jax import lax
from jax.experimental import pallas as pl
from jax.experimental.pallas import tpu as pltpu
from jax.sharding import PartitionSpec as P

MODES = 64
NY = 1024
OFFSETS = 9
BLOCK = 64
F32 = jnp.float32
BF16 = jnp.bfloat16


def basis_table(length, count):
    cells = np.arange(count, dtype=np.int64)
    waves = np.arange(MODES, dtype=np.int64)
    factor = 2.0 * math.pi / length
    cosines = np.cos((cells[:, None] * waves[None, :] % length) * factor)
    sines = np.sin((cells[:, None] * (waves[None, :] + 1) % length) * factor)
    return (2.0 / length) ** 0.5 * np.concatenate([cosines, sines], axis=1)


def two_parts(table):
    high = table.astype(jnp.bfloat16)
    low = (table - high.astype(np.float64)).astype(jnp.bfloat16)
    return high, low


def column_table():
    return np.concatenate(two_parts(np.ascontiguousarray(basis_table(NY, NY).T)), axis=0)


def row_table(devices, rows):
    table = basis_table(devices * rows, devices * rows).reshape(devices, rows * 2 * MODES)
    return np.concatenate(two_parts(table), axis=1)


def dot(left, right, left_dim=1, right_dim=0):
    return lax.dot_general(
        left, right, (((left_dim,), (right_dim,)), ((), ())), preferred_element_type=F32
    )


def call(body, outs, *args, scratch=(), flops=10**8, far=(), limit=48):
    single = isinstance(outs, tuple)
    outs = [outs] if single else outs
    shapes = [jax.ShapeDtypeStruct(*o) for o in outs]
    size = sum(
        math.prod(a.shape) * a.dtype.itemsize
        for k, a in enumerate(list(args) + shapes)
        if k not in far
    )
    result = pl.pallas_call(
        body,
        out_shape=shapes,
        in_specs=[
            pl.BlockSpec(memory_space=pltpu.HBM if k in far else pltpu.VMEM)
            for k in range(len(args))
        ],
        out_specs=[pl.BlockSpec(memory_space=pltpu.VMEM)] * len(shapes),
        scratch_shapes=list(scratch),
        compiler_params=pltpu.CompilerParams(vmem_limit_bytes=limit * 2**20),
        cost_estimate=pl.CostEstimate(flops=flops, bytes_accessed=size, transcendentals=0),
    )(*args)
    return result[0] if single else result


def every(ref, first, count, stride):
    return ref.at[pl.ds(first, count, stride=stride)]


def put_wide(wide_ref, values):
    for k in range(wide_ref.shape[0]):
        wide_ref[k] = values[:, k * 128 : (k + 1) * 128]


def get_wide(wide_ref):
    return jnp.concatenate([wide_ref[k] for k in range(wide_ref.shape[0])], axis=1)


def wide_rows(wide_ref, first, count, stride):
    return [
        wide_ref.at[k, pl.ds(first, count, stride=stride)] for k in range(wide_ref.shape[0])
    ]


def write_lines(line_ref, values, lines):
    count = values.shape[0]
    every(line_ref, 0, count, lines)[...] = values[:, :128]
    every(line_ref, 1, count, lines)[...] = values[:, 128:]


def read_lines(line_ref, count, lines):
    return jnp.concatenate(
        [every(line_ref, k, count, lines)[...].astype(BF16) for k in range(2)], axis=1
    )


def column_spread(values, table):
    both = dot(table, values, 1, 1)
    half = both.shape[0] // 2
    return both[:half] + both[half:]


def spread_body(
    field_ref, table_ref, out_ref, rows_ref, held, held_table, wide, line_ref, sems, *, rows
):
    field_copy = pltpu.make_async_copy(field_ref, held, sems.at[0])
    table_copy = pltpu.make_async_copy(table_ref, held_table, sems.at[1])
    field_copy.start()
    table_copy.start()
    field_copy.wait()
    put_wide(wide, held[...].astype(F32))
    own = rows_ref.shape[1]
    for x in range(rows):
        views = wide_rows(wide, x, own, rows)
        rows_ref[x] = jnp.concatenate([view[...] for view in views], axis=1).astype(BF16)
    table_copy.wait()
    write_lines(line_ref, column_spread(held[...], held_table[...]), 2)
    out_ref[...] = line_ref[...].astype(BF16)


def row_modes(moved, table, rows, natural):
    wide = dot(moved, table, 0, 0)
    span = wide.shape[1] // 2
    wide = wide[:, :span] + wide[:, span:]
    waves = span // rows
    count = wide.shape[0] // rows
    if natural:
        cube = wide.reshape(count, rows, span)
        place = lax.broadcasted_iota(jnp.int32, (count, rows, waves), 1)
        total = jnp.zeros((count, rows, waves), F32)
        for x in range(rows):
            total = jnp.where(place == x, cube[:, :, x * waves : (x + 1) * waves], total)
        return jnp.sum(total, axis=1)
    total = jnp.zeros((count, waves), F32)
    for x in range(rows):
        total = total + wide[x * count : (x + 1) * count, x * waves : (x + 1) * waves]
    return total


def modes_body(moved_ref, table_ref, piece_ref, ready_ref, out_ref, line_ref, *, rows):
    line_ref[...] = moved_ref[...].astype(F32)
    modes = row_modes(read_lines(line_ref, table_ref.shape[0], 2), table_ref[...], rows, True)
    own = modes.shape[0]
    for k in range(out_ref.shape[0]):
        out_ref[k, :own] = modes.astype(BF16)
        out_ref[k, own:] = piece_ref[k]


def row_values(coeffs, table, rows, natural):
    count, waves = coeffs.shape
    blocks = []
    if natural:
        spread = jnp.broadcast_to(coeffs[:, None, :], (count, rows, waves))
        place = lax.broadcasted_iota(jnp.int32, (count, rows, waves), 1)
        for x in range(rows):
            blocks.append(
                jnp.where(place == x, spread, 0.0).reshape(count * rows, waves).astype(BF16)
            )
    else:
        low = coeffs.astype(BF16)
        none = jnp.zeros((count, waves), BF16)
        for x in range(rows):
            blocks.append(jnp.concatenate([low if k == x else none for k in range(rows)], axis=0))
    placed = jnp.concatenate(blocks, axis=1)
    span = rows * waves
    return dot(table[:, :span], placed, 1, 1) + dot(table[:, span:], placed, 1, 1)


def mix_body(weight_ref, got_ref, table_ref, plain_ref, turned_ref, out_ref, line_ref, *, rows):
    waves = got_ref.shape[2]
    own = weight_ref.shape[0] // waves
    modes = got_ref[:, :own].reshape(got_ref.shape[0] * own, waves)
    lane = lax.broadcasted_iota(jnp.int32, (own, waves), 1)
    step = 8
    total = jnp.zeros((own, waves), F32)
    for first in range(0, waves, step):
        part = dot(weight_ref[first * own : (first + step) * own], modes)
        for k in range(step):
            total = jnp.where(lane == first + k, part[k * own : (k + 1) * own], total)
    write_lines(line_ref, row_values(total, table_ref[...], rows, False), 2)
    out_ref[...] = line_ref[...].astype(BF16)


def edges_body(field_ref, after_ref, low_ref, high_ref, sems):
    rows = field_ref.shape[1]
    copies = [
        pltpu.make_async_copy(field_ref.at[:, rows - 1], low_ref, sems.at[0]),
        pltpu.make_async_copy(field_ref.at[:, 0], high_ref, sems.at[1]),
    ]
    for copy in copies:
        copy.start()
    for copy in copies:
        copy.wait()


def local_body(kernel_ref, field_ref, mask_ref, out_ref, acc_ref, *, own):
    rows = field_ref.shape[1]
    channels = kernel_ref.shape[1]
    for j in range(rows):
        source = field_ref[:, j].reshape(channels, NY)
        first = 3 * max(0, j - rows + 2)
        last = 3 * min(3, j + 2)
        product = dot(kernel_ref[first * own : last * own], source)
        for t in range(first, last):
            x = j - (t // 3 - 1)
            term = product[(t - first) * own : (t - first + 1) * own] * mask_ref[
                x * OFFSETS + t : x * OFFSETS + t + 1
            ]
            slot = (x * 3 + t % 3) * own
            if t // 3 == 0 or j == 0:
                acc_ref[slot : slot + own] = term
            else:
                acc_ref[slot : slot + own] = acc_ref[slot : slot + own] + term
    for x in range(rows):
        slot = x * 3 * own
        out_ref[x * own : (x + 1) * own] = turn_back(
            [acc_ref[slot + k * own : slot + (k + 1) * own] for k in range(3)]
        )


def turn_back(parts):
    return pltpu.roll(parts[0], 1, 1) + parts[1] + pltpu.roll(parts[2], NY - 1, 1)


def slope_of(pre):
    return (
        0.5 * (1.0 + lax.erf(pre * 0.5**0.5))
        + pre * jnp.exp(-0.5 * pre * pre) * (0.5 / math.pi) ** 0.5
    )


def write_shares(line_ref, shares, lines, holders, devices):
    for k, share in enumerate(shares):
        high = share.astype(BF16).astype(F32)
        for line, value in ((2 + k, high), (5 + k, share - high)):
            every(line_ref, line, holders, lines)[...] = value
            if holders < devices:
                every(line_ref, holders * lines + line, devices - holders, lines)[...] = jnp.zeros(
                    (devices - holders, value.shape[1]), F32
                )


def grad_body(
    local_ref,
    back_ref,
    cot_ref,
    table_ref,
    field_ref,
    low_ref,
    high_ref,
    mask_ref,
    kernel_ref,
    pre_ref,
    out_ref,
    z_ref,
    back_lines,
    share_ref,
    line_ref,
    *,
    own,
    devices,
):
    rows = field_ref.shape[1]
    channels = kernel_ref.shape[1]
    back_lines[...] = back_ref[...].astype(F32)
    back = read_lines(back_lines, devices, 2)
    z_ref[...] = local_ref[...] + dot(
        jnp.concatenate([back, back], axis=0), table_ref[...], 0, 0
    )
    for x, first, ref in ((0, 0, low_ref), (rows - 1, 6, high_ref)):
        product = dot(
            kernel_ref[first * own : (first + 3) * own], ref[...].reshape(channels, NY)
        )
        parts = [
            product[k * own : (k + 1) * own]
            * mask_ref[x * OFFSETS + first + k : x * OFFSETS + first + k + 1]
            for k in range(3)
        ]
        z_ref[x * own : (x + 1) * own] = z_ref[x * own : (x + 1) * own] + turn_back(parts)
    grad = cot_ref[...].astype(F32) * slope_of(z_ref[...])
    grad_low = grad.astype(BF16)
    pre_ref[...] = grad_low
    write_lines(line_ref, column_spread(grad_low, table_ref[...]), 8)
    grad = grad_low.astype(F32)
    shifted = [
        pltpu.roll(grad, NY - 1, 1).astype(BF16),
        grad_low,
        pltpu.roll(grad, 1, 1).astype(BF16),
    ]
    total = [jnp.zeros((3 * own, channels), F32) for _ in range(3)]
    for j in range(-1, rows + 1):
        ref = low_ref if j < 0 else high_ref if j == rows else field_ref.at[:, j]
        source = ref[...].reshape(channels, NY)
        for group in range(3):
            x = j - (group - 1)
            if x < 0 or x >= rows:
                continue
            pieces = []
            for k in range(3):
                t = 3 * group + k
                pieces.append(
                    shifted[k][x * own : (x + 1) * own]
                    * mask_ref[x * OFFSETS + t : x * OFFSETS + t + 1].astype(BF16)
                )
            total[group] = total[group] + dot(jnp.concatenate(pieces, axis=0), source, 1, 1)
    for group in range(3):
        share_ref[group * 3 * own : (group + 1) * 3 * own] = total[group]
    holders = 3 * own
    write_shares(
        line_ref, [every(share_ref, k, holders, 3)[...] for k in range(3)], 8, holders, devices
    )
    out_ref[...] = line_ref[...].astype(BF16)


def back_mix_body(
    moved_ref, table_ref, weight_ref, modes_ref, out_ref, sum_ref, line_ref, *, rows, scale
):
    devices = table_ref.shape[0]
    line_ref[...] = moved_ref[...].astype(F32)
    grads = row_modes(read_lines(line_ref, devices, 8), table_ref[...], rows, False).astype(BF16)
    modes_ref[...] = grads
    own, waves = grads.shape
    turned = grads.astype(F32).T
    repeat = waves // own
    wide = jnp.concatenate([turned] * repeat, axis=1)
    lane = lax.broadcasted_iota(jnp.int32, (waves, waves), 1) // own
    row = lax.broadcasted_iota(jnp.int32, (waves, waves), 0)
    total = jnp.zeros((waves, weight_ref.shape[1]), F32)
    step = 2
    for first in range(0, own, step):
        placed = [
            jnp.where(row == repeat * (first + k) + lane, wide, 0.0).astype(BF16)
            for k in range(step)
        ]
        total = total + dot(
            jnp.concatenate(placed, axis=1),
            weight_ref[first * waves : (first + step) * waves],
        )
    out_ref[...] = total.T.astype(BF16)
    sums = line_ref[0:8]
    for r in range(1, devices):
        sums = sums + line_ref[r * 8 : (r + 1) * 8]
    sum_ref[...] = sums * scale


def back_rows_body(parts_ref, table_ref, sum_ref, *refs, rows):
    out_ref, line_ref = refs[-2:]
    parts = parts_ref[...].astype(F32)
    total = parts[0]
    for k in range(1, parts.shape[0]):
        total = total + parts[k]
    devices = table_ref.shape[0]
    write_lines(line_ref, row_values(total, table_ref[...], rows, True), 6)
    for k in range(3):
        every(line_ref, 2 + k, devices, 6)[...] = jnp.broadcast_to(
            sum_ref[2 + k : 3 + k] + sum_ref[5 + k : 6 + k], (devices, sum_ref.shape[1])
        )
    every(line_ref, 5, devices, 6)[...] = jnp.zeros((devices, sum_ref.shape[1]), F32)
    out_ref[...] = line_ref[...].astype(BF16)


def edge_back_body(kernel_ref, grad_ref, mask_ref, low_ref, high_ref, *, own):
    rows = grad_ref.shape[1]
    channels = kernel_ref.shape[1]
    for x, first, ref in ((0, 0, low_ref), (rows - 1, 6, high_ref)):
        product = dot(
            kernel_ref[first * own : (first + 3) * own], grad_ref[:, x].reshape(channels, NY)
        )
        parts = [
            product[k * own : (k + 1) * own]
            * mask_ref[x * OFFSETS + first + k : x * OFFSETS + first + k + 1]
            for k in (2, 1, 0)
        ]
        ref[...] = turn_back(parts).astype(BF16)


def local_back_body(kernel_ref, grad_ref, mask_ref, out_ref, acc_ref, *, own):
    rows = grad_ref.shape[1]
    channels = kernel_ref.shape[1]
    for x in range(rows):
        first = 3 if x == 0 else 0
        last = 6 if x == rows - 1 else 9
        product = dot(
            kernel_ref[first * own : last * own], grad_ref[:, x].reshape(channels, NY)
        )
        for t in range(first, last):
            term = product[(t - first) * own : (t - first + 1) * own] * mask_ref[
                x * OFFSETS + t : x * OFFSETS + t + 1
            ]
            slot = ((x + t // 3 - 1) * 3 + t % 3) * own
            if t // 3 == 2 or (x == 0 and t // 3 == 1):
                acc_ref[slot : slot + own] = term
            else:
                acc_ref[slot : slot + own] = acc_ref[slot : slot + own] + term
    for target in range(rows):
        slot = target * 3 * own
        value = turn_back(
            [acc_ref[slot + k * own : slot + (k + 1) * own] for k in (2, 1, 0)]
        )
        for k, view in enumerate(wide_rows(out_ref, target, own, rows)):
            view[...] = value[:, k * 128 : (k + 1) * 128]


def final_body(
    moved_ref, table_ref, local_ref, low_ref, high_ref, out_ref, share_ref, line_ref, sum_ref
):
    own = low_ref.shape[0]
    rows = local_ref.shape[1] // own
    devices = table_ref.shape[0] // 2
    holders = share_ref.shape[0] // 3
    line_ref[...] = moved_ref[...].astype(F32)
    back = read_lines(line_ref, devices, 6)
    for x, ref in ((0, low_ref), (rows - 1, high_ref)):
        edge = ref[...].astype(F32)
        for k, view in enumerate(wide_rows(sum_ref, x, own, rows)):
            view[...] = edge[:, k * 128 : (k + 1) * 128]
    for x in range(1, rows - 1):
        for view in wide_rows(sum_ref, x, own, rows):
            view[...] = jnp.zeros((own, 128), F32)
    spectral = dot(jnp.concatenate([back, back], axis=0), table_ref[...], 0, 0)
    out_ref[...] = (spectral + get_wide(local_ref) + get_wide(sum_ref)).astype(BF16)
    for k in range(3):
        every(share_ref, k, holders, 3)[...] = every(line_ref, 2 + k, holders, 6)[...]


def tile_masks(tile_ids, tile_counts):
    slots = jnp.arange(tile_ids.shape[-1], dtype=jnp.int32)
    used = slots[None, None, :] < tile_counts[:, :, None]
    labels = jnp.arange(OFFSETS, dtype=jnp.int32)
    hits = (tile_ids[:, None, :, :] == labels[None, :, None, None]) & used[:, None]
    return jnp.any(hits, axis=3).astype(BF16)


def spread_tables(blocks):
    cells = np.arange(NY)
    plain = (cells[None, :] // BLOCK == np.arange(blocks)[:, None]).astype(np.float32)
    moved = np.stack([np.roll(plain, k - 1, axis=1) for k in range(3)])
    return plain.astype(jnp.bfloat16), moved.astype(jnp.bfloat16)


def on_device(field, cotangent, local_kernel, spectral_weight, tile_ids, tile_counts):
    own, rows = field.shape[:2]
    devices = lax.axis_size("rows")
    groups = lax.axis_size("chan")
    channels = own * groups
    waves = 2 * MODES
    cells = own * rows
    table_y = jnp.asarray(column_table())
    table_x = jnp.asarray(row_table(devices, rows))
    forward = [(i, (i + 1) % devices) for i in range(devices)]
    backward = [(i, (i - 1) % devices) for i in range(devices)]
    def exchange(lines):
        count = lines.shape[0] // devices
        cube = lines.reshape(-1, count if count % 8 == 0 else 2, 128)
        moved = lax.all_to_all(cube, "rows", split_axis=0, concat_axis=0, tiled=True)
        return moved.reshape(lines.shape)

    def swap(values):
        return lax.all_to_all(values, "chan", split_axis=0, concat_axis=0, tiled=True)

    weight = spectral_weight.reshape(waves * own, channels)
    two = pltpu.VMEM((2 * devices, 128), F32)
    six = pltpu.VMEM((6 * devices, 128), F32)
    eight = pltpu.VMEM((8 * devices, 128), F32)
    wide = pltpu.VMEM((NY // 128, cells, 128), F32)
    spread, field_rows = call(
        functools.partial(spread_body, rows=rows),
        [((2 * devices, 128), BF16), ((rows, own, NY), BF16)],
        field.reshape(cells, NY),
        table_y,
        far=(0, 1),
        limit=61,
        scratch=[
            pltpu.VMEM((cells, NY), BF16),
            pltpu.VMEM(table_y.shape, BF16),
            wide,
            two,
            pltpu.SemaphoreType.DMA((2,)),
        ],
    )
    inputs = lax.all_gather(field_rows, "chan")
    moved = exchange(spread)

    pieces = jnp.transpose(local_kernel.reshape(OFFSETS, own, groups, own), (2, 0, 1, 3))
    pieces = pieces.reshape(groups, OFFSETS * own * own // 128, 128)
    kernel_lines = pieces.shape[1]
    pieces = jnp.pad(pieces, ((0, 0), (0, -kernel_lines % 16), (0, 0)))
    cot_rows = jnp.transpose(cotangent, (1, 0, 2)).reshape(cells, NY)
    plain, turned = spread_tables(tile_ids.shape[1])
    small = tile_masks(tile_ids, tile_counts)
    masks = jnp.einsum("xtb,by->xty", small, plain, preferred_element_type=F32)
    masks = masks.reshape(rows * OFFSETS, NY)
    moved_masks = jnp.einsum(
        "xgkb,kby->xgky", small.reshape(rows, 3, 3, -1), turned, preferred_element_type=F32
    ).reshape(rows * OFFSETS, NY)

    sent = call(
        functools.partial(modes_body, rows=rows),
        ((groups, own + pieces.shape[1], waves), BF16),
        moved,
        table_x,
        pieces,
        cot_rows,
        far=(3,),
        scratch=[two],
    )
    got = swap(sent)
    rows_part = call(
        functools.partial(mix_body, rows=rows),
        ((2 * devices, 128), BF16),
        weight,
        got,
        table_x,
        masks,
        moved_masks,
        far=(3, 4),
        scratch=[two],
    )
    back = exchange(rows_part)
    low, high = call(
        edges_body,
        [((groups, own, NY), BF16)] * 2,
        inputs,
        back,
        far=(0, 1),
        scratch=[pltpu.SemaphoreType.DMA((2,))],
    )
    low = lax.ppermute(low, "rows", forward)
    high = lax.ppermute(high, "rows", backward)
    kernel_rows = local_kernel.reshape(OFFSETS * own, channels)
    local = call(
        functools.partial(local_body, own=own),
        ((cells, NY), F32),
        kernel_rows,
        inputs,
        moved_masks,
        scratch=[pltpu.VMEM((rows * 3 * own, NY), F32)],
        flops=10**9,
    )
    grad_pre, grad_spread = call(
        functools.partial(grad_body, own=own, devices=devices),
        [((cells, NY), BF16), ((8 * devices, 128), BF16)],
        local,
        back,
        cot_rows,
        table_y,
        inputs,
        low,
        high,
        moved_masks,
        kernel_rows,
        scratch=[
            pltpu.VMEM((cells, NY), F32),
            two,
            pltpu.VMEM((OFFSETS * own, channels), F32),
            eight,
        ],
        flops=2 * 10**9,
    )
    all_grad = lax.all_gather(grad_pre.reshape(rows, own, NY), "chan")
    grad_moved = exchange(grad_spread)
    grad_modes, partial_in, kernel_sum = call(
        functools.partial(back_mix_body, rows=rows, scale=(devices * rows * NY) ** (-0.5)),
        [((own, waves), BF16), ((channels, waves), BF16), ((8, channels), F32)],
        grad_moved,
        table_x,
        weight,
        scratch=[eight],
    )
    parts_in = swap(partial_in.reshape(groups, own, waves))
    all_modes = got[:, :own].reshape(channels, waves)
    kernel_back = (
        jnp.transpose(
            got[:, own : own + kernel_lines].reshape(groups, OFFSETS, own, own), (1, 3, 0, 2)
        )
    ).reshape(OFFSETS * own, channels)
    left = jnp.transpose(grad_modes).astype(F32)
    right = jnp.transpose(all_modes).astype(F32)
    grad_spectral = (left[None, :, :, None] * right[None, :, None, :]).astype(BF16)
    back_part = call(
        functools.partial(back_rows_body, rows=rows),
        ((6 * devices, 128), BF16),
        parts_in,
        table_x,
        kernel_sum,
        grad_spectral,
        kernel_back,
        far=(3, 4),
        scratch=[six],
    )
    final = exchange(back_part)
    to_low, to_high = call(
        functools.partial(edge_back_body, own=own),
        [((own, NY), BF16), ((own, NY), BF16)],
        kernel_back,
        all_grad,
        masks,
        flops=10**8,
    )
    from_high = lax.ppermute(to_low, "rows", backward)
    from_low = lax.ppermute(to_high, "rows", forward)
    local_back = call(
        functools.partial(local_back_body, own=own),
        ((NY // 128, cells, 128), F32),
        kernel_back,
        all_grad,
        masks,
        scratch=[pltpu.VMEM((rows * 3 * own, NY), F32)],
        flops=10**9,
    )
    grad_field, grad_kernel = call(
        final_body,
        [((cells, NY), BF16), ((OFFSETS * own, channels), F32)],
        final,
        table_y,
        local_back,
        from_low,
        from_high,
        scratch=[six, wide],
    )
    return (
        grad_field.reshape(own, rows, NY),
        grad_spectral,
        grad_kernel.reshape(OFFSETS, own, channels),
    )


def solution(mesh):
    placed = (
        P("chan", "rows", None),
        P("chan", "rows", None),
        P(None, "chan", None),
        P("rows", None, "chan", None),
        P("rows", None, None),
        P("rows", None),
    )
    return jax.shard_map(
        on_device,
        mesh=mesh,
        in_specs=placed,
        out_specs=(P("chan", "rows", None), P("rows", None, "chan", None), P(None, "chan", None)),
        check_vma=False,
    )
```

```python
import functools
import math

import jax
import jax.numpy as jnp
import numpy as np
from jax import lax
from jax.experimental import pallas as pl
from jax.experimental.pallas import tpu as pltpu
from jax.sharding import PartitionSpec as P

MODES = 64
NY = 1024
OFFSETS = 9
BLOCK = 64
F32 = jnp.float32
BF16 = jnp.bfloat16


def basis_table(length, count):
    cells = np.arange(count, dtype=np.int64)
    waves = np.arange(MODES, dtype=np.int64)
    factor = 2.0 * math.pi / length
    cosines = np.cos((cells[:, None] * waves[None, :] % length) * factor)
    sines = np.sin((cells[:, None] * (waves[None, :] + 1) % length) * factor)
    return (2.0 / length) ** 0.5 * np.concatenate([cosines, sines], axis=1)


def two_parts(table):
    high = table.astype(jnp.bfloat16)
    low = (table - high.astype(np.float64)).astype(jnp.bfloat16)
    return high, low


def column_table():
    return np.concatenate(two_parts(np.ascontiguousarray(basis_table(NY, NY).T)), axis=0)


def row_table(devices, rows):
    table = basis_table(devices * rows, devices * rows).reshape(devices, rows * 2 * MODES)
    return np.concatenate(two_parts(table), axis=1)


def dot(left, right, left_dim=1, right_dim=0):
    return lax.dot_general(
        left, right, (((left_dim,), (right_dim,)), ((), ())), preferred_element_type=F32
    )


def call(body, outs, *args, scratch=(), flops=10**8, far=(), limit=48):
    single = isinstance(outs, tuple)
    outs = [outs] if single else outs
    shapes = [jax.ShapeDtypeStruct(*o) for o in outs]
    size = sum(
        math.prod(a.shape) * a.dtype.itemsize
        for k, a in enumerate(list(args) + shapes)
        if k not in far
    )
    result = pl.pallas_call(
        body,
        out_shape=shapes,
        in_specs=[
            pl.BlockSpec(memory_space=pltpu.HBM if k in far else pltpu.VMEM)
            for k in range(len(args))
        ],
        out_specs=[pl.BlockSpec(memory_space=pltpu.VMEM)] * len(shapes),
        scratch_shapes=list(scratch),
        compiler_params=pltpu.CompilerParams(vmem_limit_bytes=limit * 2**20),
        cost_estimate=pl.CostEstimate(flops=flops, bytes_accessed=size, transcendentals=0),
    )(*args)
    return result[0] if single else result


def every(ref, first, count, stride):
    return ref.at[pl.ds(first, count, stride=stride)]


def put_wide(wide_ref, values):
    for k in range(wide_ref.shape[0]):
        wide_ref[k] = values[:, k * 128 : (k + 1) * 128]


def get_wide(wide_ref):
    return jnp.concatenate([wide_ref[k] for k in range(wide_ref.shape[0])], axis=1)


def wide_rows(wide_ref, first, count, stride):
    return [
        wide_ref.at[k, pl.ds(first, count, stride=stride)] for k in range(wide_ref.shape[0])
    ]


def write_lines(line_ref, values, lines):
    count = values.shape[0]
    every(line_ref, 0, count, lines)[...] = values[:, :128]
    every(line_ref, 1, count, lines)[...] = values[:, 128:]


def read_lines(line_ref, count, lines):
    return jnp.concatenate(
        [every(line_ref, k, count, lines)[...].astype(BF16) for k in range(2)], axis=1
    )


def column_spread(values, table):
    both = dot(table, values, 1, 1)
    half = both.shape[0] // 2
    return both[:half] + both[half:]


def spread_body(
    field_ref, table_ref, out_ref, rows_ref, held, held_table, wide, line_ref, sems, *, rows
):
    field_copy = pltpu.make_async_copy(field_ref, held, sems.at[0])
    table_copy = pltpu.make_async_copy(table_ref, held_table, sems.at[1])
    field_copy.start()
    table_copy.start()
    field_copy.wait()
    put_wide(wide, held[...].astype(F32))
    own = rows_ref.shape[1]
    for x in range(rows):
        views = wide_rows(wide, x, own, rows)
        rows_ref[x] = jnp.concatenate([view[...] for view in views], axis=1).astype(BF16)
    table_copy.wait()
    write_lines(line_ref, column_spread(held[...], held_table[...]), 2)
    out_ref[...] = line_ref[...].astype(BF16)


def row_modes(moved, table, rows, natural):
    wide = dot(moved, table, 0, 0)
    span = wide.shape[1] // 2
    wide = wide[:, :span] + wide[:, span:]
    waves = span // rows
    count = wide.shape[0] // rows
    if natural:
        cube = wide.reshape(count, rows, span)
        place = lax.broadcasted_iota(jnp.int32, (count, rows, waves), 1)
        total = jnp.zeros((count, rows, waves), F32)
        for x in range(rows):
            total = jnp.where(place == x, cube[:, :, x * waves : (x + 1) * waves], total)
        return jnp.sum(total, axis=1)
    total = jnp.zeros((count, waves), F32)
    for x in range(rows):
        total = total + wide[x * count : (x + 1) * count, x * waves : (x + 1) * waves]
    return total


def modes_body(moved_ref, table_ref, piece_ref, ready_ref, out_ref, line_ref, *, rows):
    line_ref[...] = moved_ref[...].astype(F32)
    modes = row_modes(read_lines(line_ref, table_ref.shape[0], 2), table_ref[...], rows, True)
    own = modes.shape[0]
    for k in range(out_ref.shape[0]):
        out_ref[k, :own] = modes.astype(BF16)
        out_ref[k, own:] = piece_ref[k]


def row_values(coeffs, table, rows, natural):
    count, waves = coeffs.shape
    blocks = []
    if natural:
        spread = jnp.broadcast_to(coeffs[:, None, :], (count, rows, waves))
        place = lax.broadcasted_iota(jnp.int32, (count, rows, waves), 1)
        for x in range(rows):
            blocks.append(
                jnp.where(place == x, spread, 0.0).reshape(count * rows, waves).astype(BF16)
            )
    else:
        low = coeffs.astype(BF16)
        none = jnp.zeros((count, waves), BF16)
        for x in range(rows):
            blocks.append(jnp.concatenate([low if k == x else none for k in range(rows)], axis=0))
    placed = jnp.concatenate(blocks, axis=1)
    span = rows * waves
    return dot(table[:, :span], placed, 1, 1) + dot(table[:, span:], placed, 1, 1)


def mix_body(weight_ref, got_ref, table_ref, plain_ref, turned_ref, out_ref, line_ref, *, rows):
    waves = got_ref.shape[2]
    own = weight_ref.shape[0] // waves
    modes = got_ref[:, :own].reshape(got_ref.shape[0] * own, waves)
    lane = lax.broadcasted_iota(jnp.int32, (own, waves), 1)
    step = 8
    total = jnp.zeros((own, waves), F32)
    for first in range(0, waves, step):
        part = dot(weight_ref[first * own : (first + step) * own], modes)
        for k in range(step):
            total = jnp.where(lane == first + k, part[k * own : (k + 1) * own], total)
    write_lines(line_ref, row_values(total, table_ref[...], rows, False), 2)
    out_ref[...] = line_ref[...].astype(BF16)


def edges_body(field_ref, after_ref, low_ref, high_ref, sems):
    rows = field_ref.shape[1]
    copies = [
        pltpu.make_async_copy(field_ref.at[:, rows - 1], low_ref, sems.at[0]),
        pltpu.make_async_copy(field_ref.at[:, 0], high_ref, sems.at[1]),
    ]
    for copy in copies:
        copy.start()
    for copy in copies:
        copy.wait()


def local_body(kernel_ref, field_ref, mask_ref, out_ref, acc_ref, *, own):
    rows = field_ref.shape[1]
    channels = kernel_ref.shape[1]
    for j in range(rows):
        source = field_ref[:, j].reshape(channels, NY)
        first = 3 * max(0, j - rows + 2)
        last = 3 * min(3, j + 2)
        product = dot(kernel_ref[first * own : last * own], source)
        for t in range(first, last):
            x = j - (t // 3 - 1)
            term = product[(t - first) * own : (t - first + 1) * own] * mask_ref[
                x * OFFSETS + t : x * OFFSETS + t + 1
            ]
            slot = (x * 3 + t % 3) * own
            if t // 3 == 0 or j == 0:
                acc_ref[slot : slot + own] = term
            else:
                acc_ref[slot : slot + own] = acc_ref[slot : slot + own] + term
    for x in range(rows):
        slot = x * 3 * own
        out_ref[x * own : (x + 1) * own] = turn_back(
            [acc_ref[slot + k * own : slot + (k + 1) * own] for k in range(3)]
        )


def turn_back(parts):
    return pltpu.roll(parts[0], 1, 1) + parts[1] + pltpu.roll(parts[2], NY - 1, 1)


def slope_of(pre):
    return (
        0.5 * (1.0 + lax.erf(pre * 0.5**0.5))
        + pre * jnp.exp(-0.5 * pre * pre) * (0.5 / math.pi) ** 0.5
    )


def write_shares(line_ref, shares, lines, holders, devices):
    for k, share in enumerate(shares):
        high = share.astype(BF16).astype(F32)
        for line, value in ((2 + k, high), (5 + k, share - high)):
            every(line_ref, line, holders, lines)[...] = value
            if holders < devices:
                every(line_ref, holders * lines + line, devices - holders, lines)[...] = jnp.zeros(
                    (devices - holders, value.shape[1]), F32
                )


def grad_body(
    local_ref,
    back_ref,
    cot_ref,
    table_ref,
    field_ref,
    low_ref,
    high_ref,
    mask_ref,
    kernel_ref,
    pre_ref,
    out_ref,
    z_ref,
    back_lines,
    share_ref,
    line_ref,
    *,
    own,
    devices,
):
    rows = field_ref.shape[1]
    channels = kernel_ref.shape[1]
    back_lines[...] = back_ref[...].astype(F32)
    back = read_lines(back_lines, devices, 2)
    z_ref[...] = local_ref[...] + dot(
        jnp.concatenate([back, back], axis=0), table_ref[...], 0, 0
    )
    for x, first, ref in ((0, 0, low_ref), (rows - 1, 6, high_ref)):
        product = dot(
            kernel_ref[first * own : (first + 3) * own], ref[...].reshape(channels, NY)
        )
        parts = [
            product[k * own : (k + 1) * own]
            * mask_ref[x * OFFSETS + first + k : x * OFFSETS + first + k + 1]
            for k in range(3)
        ]
        z_ref[x * own : (x + 1) * own] = z_ref[x * own : (x + 1) * own] + turn_back(parts)
    grad = cot_ref[...].astype(F32) * slope_of(z_ref[...])
    grad_low = grad.astype(BF16)
    pre_ref[...] = grad_low
    write_lines(line_ref, column_spread(grad_low, table_ref[...]), 8)
    grad = grad_low.astype(F32)
    shifted = [
        pltpu.roll(grad, NY - 1, 1).astype(BF16),
        grad_low,
        pltpu.roll(grad, 1, 1).astype(BF16),
    ]
    total = [jnp.zeros((3 * own, channels), F32) for _ in range(3)]
    for j in range(-1, rows + 1):
        ref = low_ref if j < 0 else high_ref if j == rows else field_ref.at[:, j]
        source = ref[...].reshape(channels, NY)
        for group in range(3):
            x = j - (group - 1)
            if x < 0 or x >= rows:
                continue
            pieces = []
            for k in range(3):
                t = 3 * group + k
                pieces.append(
                    shifted[k][x * own : (x + 1) * own]
                    * mask_ref[x * OFFSETS + t : x * OFFSETS + t + 1].astype(BF16)
                )
            total[group] = total[group] + dot(jnp.concatenate(pieces, axis=0), source, 1, 1)
    for group in range(3):
        share_ref[group * 3 * own : (group + 1) * 3 * own] = total[group]
    holders = 3 * own
    write_shares(
        line_ref, [every(share_ref, k, holders, 3)[...] for k in range(3)], 8, holders, devices
    )
    out_ref[...] = line_ref[...].astype(BF16)


def back_mix_body(
    moved_ref, table_ref, weight_ref, modes_ref, out_ref, sum_ref, line_ref, *, rows, scale
):
    devices = table_ref.shape[0]
    line_ref[...] = moved_ref[...].astype(F32)
    grads = row_modes(read_lines(line_ref, devices, 8), table_ref[...], rows, False).astype(BF16)
    modes_ref[...] = grads
    own, waves = grads.shape
    turned = grads.astype(F32).T
    repeat = waves // own
    wide = jnp.concatenate([turned] * repeat, axis=1)
    lane = lax.broadcasted_iota(jnp.int32, (waves, waves), 1) // own
    row = lax.broadcasted_iota(jnp.int32, (waves, waves), 0)
    total = jnp.zeros((waves, weight_ref.shape[1]), F32)
    step = 2
    for first in range(0, own, step):
        placed = [
            jnp.where(row == repeat * (first + k) + lane, wide, 0.0).astype(BF16)
            for k in range(step)
        ]
        total = total + dot(
            jnp.concatenate(placed, axis=1),
            weight_ref[first * waves : (first + step) * waves],
        )
    out_ref[...] = total.T.astype(BF16)
    sums = line_ref[0:8]
    for r in range(1, devices):
        sums = sums + line_ref[r * 8 : (r + 1) * 8]
    sum_ref[...] = sums * scale


def back_rows_body(parts_ref, table_ref, sum_ref, *refs, rows):
    out_ref, line_ref = refs[-2:]
    parts = parts_ref[...].astype(F32)
    total = parts[0]
    for k in range(1, parts.shape[0]):
        total = total + parts[k]
    devices = table_ref.shape[0]
    write_lines(line_ref, row_values(total, table_ref[...], rows, True), 6)
    for k in range(3):
        every(line_ref, 2 + k, devices, 6)[...] = jnp.broadcast_to(
            sum_ref[2 + k : 3 + k] + sum_ref[5 + k : 6 + k], (devices, sum_ref.shape[1])
        )
    every(line_ref, 5, devices, 6)[...] = jnp.zeros((devices, sum_ref.shape[1]), F32)
    out_ref[...] = line_ref[...].astype(BF16)


def edge_back_body(kernel_ref, grad_ref, mask_ref, low_ref, high_ref, *, own):
    rows = grad_ref.shape[1]
    channels = kernel_ref.shape[1]
    for x, first, ref in ((0, 0, low_ref), (rows - 1, 6, high_ref)):
        product = dot(
            kernel_ref[first * own : (first + 3) * own], grad_ref[:, x].reshape(channels, NY)
        )
        parts = [
            product[k * own : (k + 1) * own]
            * mask_ref[x * OFFSETS + first + k : x * OFFSETS + first + k + 1]
            for k in (2, 1, 0)
        ]
        ref[...] = turn_back(parts).astype(BF16)


def local_back_body(kernel_ref, grad_ref, mask_ref, out_ref, acc_ref, *, own):
    rows = grad_ref.shape[1]
    channels = kernel_ref.shape[1]
    for x in range(rows):
        first = 3 if x == 0 else 0
        last = 6 if x == rows - 1 else 9
        product = dot(
            kernel_ref[first * own : last * own], grad_ref[:, x].reshape(channels, NY)
        )
        for t in range(first, last):
            term = product[(t - first) * own : (t - first + 1) * own] * mask_ref[
                x * OFFSETS + t : x * OFFSETS + t + 1
            ]
            slot = ((x + t // 3 - 1) * 3 + t % 3) * own
            if t // 3 == 2 or (x == 0 and t // 3 == 1):
                acc_ref[slot : slot + own] = term
            else:
                acc_ref[slot : slot + own] = acc_ref[slot : slot + own] + term
    for target in range(rows):
        slot = target * 3 * own
        value = turn_back(
            [acc_ref[slot + k * own : slot + (k + 1) * own] for k in (2, 1, 0)]
        )
        for k, view in enumerate(wide_rows(out_ref, target, own, rows)):
            view[...] = value[:, k * 128 : (k + 1) * 128]


def final_body(
    moved_ref, table_ref, local_ref, low_ref, high_ref, out_ref, share_ref, line_ref, sum_ref
):
    own = low_ref.shape[0]
    rows = local_ref.shape[1] // own
    devices = table_ref.shape[0] // 2
    holders = share_ref.shape[0] // 3
    line_ref[...] = moved_ref[...].astype(F32)
    back = read_lines(line_ref, devices, 6)
    for x, ref in ((0, low_ref), (rows - 1, high_ref)):
        edge = ref[...].astype(F32)
        for k, view in enumerate(wide_rows(sum_ref, x, own, rows)):
            view[...] = edge[:, k * 128 : (k + 1) * 128]
    for x in range(1, rows - 1):
        for view in wide_rows(sum_ref, x, own, rows):
            view[...] = jnp.zeros((own, 128), F32)
    spectral = dot(jnp.concatenate([back, back], axis=0), table_ref[...], 0, 0)
    out_ref[...] = (spectral + get_wide(local_ref) + get_wide(sum_ref)).astype(BF16)
    for k in range(3):
        every(share_ref, k, holders, 3)[...] = every(line_ref, 2 + k, holders, 6)[...]


def tile_masks(tile_ids, tile_counts):
    slots = jnp.arange(tile_ids.shape[-1], dtype=jnp.int32)
    used = slots[None, None, :] < tile_counts[:, :, None]
    labels = jnp.arange(OFFSETS, dtype=jnp.int32)
    hits = (tile_ids[:, None, :, :] == labels[None, :, None, None]) & used[:, None]
    return jnp.any(hits, axis=3).astype(BF16)


def spread_tables(blocks):
    cells = np.arange(NY)
    plain = (cells[None, :] // BLOCK == np.arange(blocks)[:, None]).astype(np.float32)
    moved = np.stack([np.roll(plain, k - 1, axis=1) for k in range(3)])
    return plain.astype(jnp.bfloat16), moved.astype(jnp.bfloat16)


def on_device(field, cotangent, local_kernel, spectral_weight, tile_ids, tile_counts):
    own, rows = field.shape[:2]
    devices = lax.axis_size("rows")
    groups = lax.axis_size("chan")
    channels = own * groups
    waves = 2 * MODES
    cells = own * rows
    table_y = jnp.asarray(column_table())
    table_x = jnp.asarray(row_table(devices, rows))
    forward = [(i, (i + 1) % devices) for i in range(devices)]
    backward = [(i, (i - 1) % devices) for i in range(devices)]
    def exchange(lines):
        count = lines.shape[0] // devices
        cube = lines.reshape(-1, count if count % 8 == 0 else 2, 128)
        moved = lax.all_to_all(cube, "rows", split_axis=0, concat_axis=0, tiled=True)
        return moved.reshape(lines.shape)

    def swap(values):
        return lax.all_to_all(values, "chan", split_axis=0, concat_axis=0, tiled=True)

    weight = spectral_weight.reshape(waves * own, channels)
    two = pltpu.VMEM((2 * devices, 128), F32)
    six = pltpu.VMEM((6 * devices, 128), F32)
    eight = pltpu.VMEM((8 * devices, 128), F32)
    wide = pltpu.VMEM((NY // 128, cells, 128), F32)
    spread, field_rows = call(
        functools.partial(spread_body, rows=rows),
        [((2 * devices, 128), BF16), ((rows, own, NY), BF16)],
        field.reshape(cells, NY),
        table_y,
        far=(0, 1),
        limit=61,
        scratch=[
            pltpu.VMEM((cells, NY), BF16),
            pltpu.VMEM(table_y.shape, BF16),
            wide,
            two,
            pltpu.SemaphoreType.DMA((2,)),
        ],
    )
    inputs = lax.all_gather(field_rows, "chan")
    moved = exchange(spread)

    pieces = jnp.transpose(local_kernel.reshape(OFFSETS, own, groups, own), (2, 0, 1, 3))
    pieces = pieces.reshape(groups, OFFSETS * own * own // 128, 128)
    kernel_lines = pieces.shape[1]
    pieces = jnp.pad(pieces, ((0, 0), (0, -kernel_lines % 16), (0, 0)))
    cot_rows = jnp.transpose(cotangent, (1, 0, 2)).reshape(cells, NY)
    plain, turned = spread_tables(tile_ids.shape[1])
    small = tile_masks(tile_ids, tile_counts)
    masks = jnp.einsum("xtb,by->xty", small, plain, preferred_element_type=F32)
    masks = masks.reshape(rows * OFFSETS, NY)
    moved_masks = jnp.einsum(
        "xgkb,kby->xgky", small.reshape(rows, 3, 3, -1), turned, preferred_element_type=F32
    ).reshape(rows * OFFSETS, NY)

    sent = call(
        functools.partial(modes_body, rows=rows),
        ((groups, own + pieces.shape[1], waves), BF16),
        moved,
        table_x,
        pieces,
        cot_rows,
        far=(3,),
        scratch=[two],
    )
    got = swap(sent)
    rows_part = call(
        functools.partial(mix_body, rows=rows),
        ((2 * devices, 128), BF16),
        weight,
        got,
        table_x,
        masks,
        moved_masks,
        far=(3, 4),
        scratch=[two],
    )
    back = exchange(rows_part)
    low, high = call(
        edges_body,
        [((groups, own, NY), BF16)] * 2,
        inputs,
        back,
        far=(0, 1),
        scratch=[pltpu.SemaphoreType.DMA((2,))],
    )
    low = lax.ppermute(low, "rows", forward)
    high = lax.ppermute(high, "rows", backward)
    kernel_rows = local_kernel.reshape(OFFSETS * own, channels)
    local = call(
        functools.partial(local_body, own=own),
        ((cells, NY), F32),
        kernel_rows,
        inputs,
        moved_masks,
        scratch=[pltpu.VMEM((rows * 3 * own, NY), F32)],
        flops=10**9,
    )
    grad_pre, grad_spread = call(
        functools.partial(grad_body, own=own, devices=devices),
        [((cells, NY), BF16), ((8 * devices, 128), BF16)],
        local,
        back,
        cot_rows,
        table_y,
        inputs,
        low,
        high,
        moved_masks,
        kernel_rows,
        scratch=[
            pltpu.VMEM((cells, NY), F32),
            two,
            pltpu.VMEM((OFFSETS * own, channels), F32),
            eight,
        ],
        limit=57,
        flops=2 * 10**9,
    )
    all_grad = lax.all_gather(grad_pre.reshape(rows, own, NY), "chan")
    grad_moved = exchange(grad_spread)
    grad_modes, partial_in, kernel_sum = call(
        functools.partial(back_mix_body, rows=rows, scale=(devices * rows * NY) ** (-0.5)),
        [((own, waves), BF16), ((channels, waves), BF16), ((8, channels), F32)],
        grad_moved,
        table_x,
        weight,
        scratch=[eight],
    )
    parts_in = swap(partial_in.reshape(groups, own, waves))
    all_modes = got[:, :own].reshape(channels, waves)
    kernel_back = (
        jnp.transpose(
            got[:, own : own + kernel_lines].reshape(groups, OFFSETS, own, own), (1, 3, 0, 2)
        )
    ).reshape(OFFSETS * own, channels)
    left = jnp.transpose(grad_modes).astype(F32)
    right = jnp.transpose(all_modes).astype(F32)
    grad_spectral = (left[None, :, :, None] * right[None, :, None, :]).astype(BF16)
    back_part = call(
        functools.partial(back_rows_body, rows=rows),
        ((6 * devices, 128), BF16),
        parts_in,
        table_x,
        kernel_sum,
        grad_spectral,
        kernel_back,
        far=(3, 4),
        scratch=[six],
    )
    final = exchange(back_part)
    to_low, to_high = call(
        functools.partial(edge_back_body, own=own),
        [((own, NY), BF16), ((own, NY), BF16)],
        kernel_back,
        all_grad,
        masks,
        flops=10**8,
    )
    from_high = lax.ppermute(to_low, "rows", backward)
    from_low = lax.ppermute(to_high, "rows", forward)
    local_back = call(
        functools.partial(local_back_body, own=own),
        ((NY // 128, cells, 128), F32),
        kernel_back,
        all_grad,
        masks,
        scratch=[pltpu.VMEM((rows * 3 * own, NY), F32)],
        flops=10**9,
    )
    grad_field, grad_kernel = call(
        final_body,
        [((cells, NY), BF16), ((OFFSETS * own, channels), F32)],
        final,
        table_y,
        local_back,
        from_low,
        from_high,
        scratch=[six, wide],
    )
    return (
        grad_field.reshape(own, rows, NY),
        grad_spectral,
        grad_kernel.reshape(OFFSETS, own, channels),
    )


def solution(mesh):
    placed = (
        P("chan", "rows", None),
        P("chan", "rows", None),
        P(None, "chan", None),
        P("rows", None, "chan", None),
        P("rows", None, None),
        P("rows", None),
    )
    return jax.shard_map(
        on_device,
        mesh=mesh,
        in_specs=placed,
        out_specs=(P("chan", "rows", None), P("rows", None, "chan", None), P(None, "chan", None)),
        check_vma=False,
    )
```
